32 devices in a mesh: groups: 2 (over y), tile: 4 (over z), face: 4 (over x, core).
Axes of the slice: x: 2, y: 2, z: 4, core: 2. Of those that a mesh axis runs over, the one named last changes fastest.
Arguments:
- noisy_state: float32 [24, 256, 512], P('groups', 'face', 'tile'), parts along dimension 0, may hold values from -6 to 6
- conditioning: float32 [24, 256, 512], P('groups', 'face', 'tile'), parts along dimension 0, may hold values from -6 to 6
- orient: int32 [4, 8], replicated, may hold values from 0 to 3
- corner_points: int32 [4, 8], replicated, may hold values 0 or 1
- w_state: bfloat16 [128, 108], replicated, may hold values from -0.625 to 0.625
- w_cond: bfloat16 [128, 108], replicated, may hold values from -0.625 to 0.625
- w_out: bfloat16 [108, 128], replicated, may hold values from -0.1875 to 0.1875
- embed_first: float32 [128], replicated, may hold values from -3 to 3
- embed_second: float32 [128], replicated, may hold values from -3 to 3
Outputs:
- next_state: float32 [24, 256, 512], P('groups', 'face', 'tile'), parts along dimension 0
The draws below stay inside these ranges and needn't reach their ends.
There are 2 independent parts, one for each index of `groups`. The reference program is written for one: setup_inputs(seed, part) draws one part's arguments, and reference() takes and returns one part's arrays. A program takes and returns all parts, laid end to end along the dimension named above; an argument that names none is the same for every part. Nothing has to cross between parts.
Inputs may be any that keep to these rules, and one draw needn't show every extreme that they name: `orient`: A tile's stored pixels are its pixels in the grid's frame turned by this many quarter turns. `corner_points`: entry (r, c) belongs to the upper-left corner of tile (r, c).
All inputs are finite; a program needn't handle non-finite values.
Results may differ from the reference program's by a relative error of at most 0.0019.
Values sent between devices are 32-bit elements; how exact they have to be, the bound alone decides.
A program may use at most 256 MiB of HBM per device.

```python
import math
import jax
import jax.numpy as jnp
from jax import lax

FIELDS = 12
HIDDEN_SIZE = 128
P_SIZE = 64
RIM = 8
NR = 4
NC = 8
ROWS = 256
COLS = 512


def with_ends(result, key, smallest, largest):
    place = [jax.random.randint(jax.random.fold_in(key, axis), (), 0, length) for axis, length in enumerate(result.shape)]
    main_axis = result.shape.index(max(result.shape))
    beside = place[:main_axis] + [(place[main_axis] + 1) % result.shape[main_axis]] + place[main_axis + 1:]
    return result.at[tuple(place)].set(smallest).at[tuple(beside)].set(largest)


def block_levels(own_key, shape, cuts, least, high):
    factor_of = 1.0
    for dim, blocks in cuts:
        draws = jax.random.uniform(jax.random.fold_in(jax.random.fold_in(own_key, 6), dim), (blocks,), jnp.float32, least / len(cuts), high / len(cuts))
        factor_of = factor_of * jnp.repeat(jnp.exp(draws), shape[dim] // blocks).reshape((-1,) + (1,) * (len(shape) - 1 - dim))
    return factor_of


def centred(stream_key, shape, scale, most, split=(), kind=jnp.bfloat16):
    drawn = jax.random.normal(stream_key, shape, jnp.float32) * scale
    if len(split) > 0:
        drawn = block_levels(stream_key, shape, split, -0.22, 0.18) * drawn
    return jnp.clip(drawn, min=-most, max=most).astype(kind)


def setup_inputs(seed: int = 0, part: int = 0) -> dict:
    seeds = jax.random.split(jax.random.key(seed), 10)
    own_keys = jax.random.split(jax.random.fold_in(seeds[9], part), 10)
    return {
        "noisy_state": centred(own_keys[0], (FIELDS, ROWS, COLS), 1.0, 6.0, ((1, 4), (2, 4)), jnp.float32),
        "conditioning": centred(own_keys[1], (FIELDS, ROWS, COLS), 1.0, 6.0, ((1, 4), (2, 4)), jnp.float32),
        "orient": with_ends(jax.random.randint(seeds[2], (NR, NC), 0, 4), jax.random.fold_in(seeds[2], 1), 0, 3).astype(jnp.int32),
        "corner_points": with_ends((jax.random.randint(seeds[3], (NR, NC), 0, 8) < 1).astype(jnp.int32), jax.random.fold_in(seeds[3], 1), 0, 1),
        "w_state": centred(seeds[4], (HIDDEN_SIZE, 9 * FIELDS), (9 * FIELDS) ** -0.5, 0.625),
        "w_cond": centred(seeds[5], (HIDDEN_SIZE, 9 * FIELDS), (9 * FIELDS) ** -0.5, 0.625),
        "w_out": centred(seeds[6], (9 * FIELDS, HIDDEN_SIZE), (9 * HIDDEN_SIZE) ** -0.5, 0.1875),
        "embed_first": centred(seeds[7], (HIDDEN_SIZE,), 0.5, 3.0, (), jnp.float32),
        "embed_second": centred(seeds[8], (HIDDEN_SIZE,), 0.5, 3.0, (), jnp.float32),
    }


guide_weight = 2.0
sigma_first = 1.0
sigma_second = 0.6
step_size = sigma_second - sigma_first
scale_first = 1.0 / math.sqrt(1.0 + sigma_first ** 2)
scale_second = 1.0 / math.sqrt(1.0 + sigma_second ** 2)

def rotate_by(picture, quarters):
    turned = jnp.stack([jnp.rot90(picture, quarter, axes=(-2, -1)) for quarter in range(4)])
    return turned[quarters]

def patches(picture):
    channels, height, breadth = picture.shape
    padded = jnp.pad(picture, ((0, 0), (1, 1), (1, 1)))
    stacked = jnp.concatenate([padded[:, row_step:row_step + height, col_step:col_step + breadth] for row_step in range(3) for col_step in range(3)], axis=0)
    return stacked.reshape(9 * channels, height * breadth)

def spread(products, channels, height, breadth):
    shaped = products.reshape(9, channels, height, breadth)
    padded = jnp.pad(shaped, ((0, 0), (0, 0), (1, 1), (1, 1)))
    summed = jnp.zeros((channels, height, breadth), jnp.float32)
    for row_step in range(3):
        for col_step in range(3):
            summed = summed + padded[3 * row_step + col_step, :, row_step:row_step + height, col_step:col_step + breadth]
    return summed

def predict(own_frame, feature, w_state, w_out, embedding, input_scale):
    channels, height, breadth = own_frame.shape
    lowered = (input_scale * own_frame).astype(jnp.bfloat16)
    mixed_sum = jnp.dot(w_state, patches(lowered), preferred_element_type=jnp.float32) + embedding[:, None]
    plain_hidden = jax.nn.silu(mixed_sum).astype(jnp.bfloat16)
    cond_hidden = jax.nn.silu(mixed_sum + feature).astype(jnp.bfloat16)
    plain_prod = jnp.dot(w_out, plain_hidden, preferred_element_type=jnp.float32)
    cond_prod = jnp.dot(w_out, cond_hidden, preferred_element_type=jnp.float32)
    return spread(plain_prod + guide_weight * (cond_prod - plain_prod), channels, height, breadth)

def corner_flags(corner_points, tile_row, tile_col):
    grid_rows, grid_cols = corner_points.shape
    next_row = (tile_row + 1) % grid_rows
    next_col = (tile_col + 1) % grid_cols
    return (corner_points[tile_row, tile_col], corner_points[tile_row, next_col], corner_points[next_row, tile_col], corner_points[next_row, next_col])

def corner_keep(corner_cut, tile_side):
    extent = tile_side + 2 * RIM
    row_ids = jnp.arange(extent, dtype=jnp.int32)[:, None]
    col_ids = jnp.arange(extent, dtype=jnp.int32)[None, :]
    upper_band = row_ids < RIM
    lower_band = row_ids >= tile_side + RIM
    left_side = col_ids < RIM
    right_side = col_ids >= tile_side + RIM
    dropped = upper_band & left_side & (corner_cut[0] == 1) | upper_band & right_side & (corner_cut[1] == 1) | lower_band & left_side & (corner_cut[2] == 1) | lower_band & right_side & (corner_cut[3] == 1)
    return jnp.where(dropped, 0.0, 1.0).astype(jnp.float32)

def coverage_of(local_row, local_col, corner_cut, tile_side):
    upper_band = local_row < RIM
    lower_band = local_row >= tile_side - RIM
    left_side = local_col < RIM
    right_side = local_col >= tile_side - RIM
    edge_hits = upper_band.astype(jnp.float32) + lower_band.astype(jnp.float32) + left_side.astype(jnp.float32) + right_side.astype(jnp.float32)
    diagonal = (upper_band & left_side & (corner_cut[0] == 0)).astype(jnp.float32)
    diagonal = diagonal + (upper_band & right_side & (corner_cut[1] == 0)).astype(jnp.float32)
    diagonal = diagonal + (lower_band & left_side & (corner_cut[2] == 0)).astype(jnp.float32)
    diagonal = diagonal + (lower_band & right_side & (corner_cut[3] == 0)).astype(jnp.float32)
    return 1.0 + edge_hits + diagonal

def reframe(field_data, turn_codes):
    fields = field_data.shape[0]
    blocks = field_data.reshape(fields, NR, P_SIZE, NC, P_SIZE).transpose(1, 3, 0, 2, 4).reshape(NR * NC, fields, P_SIZE, P_SIZE)

    def turn_one(pieces):
        return rotate_by(pieces[0], pieces[1])
    turned = lax.map(turn_one, (blocks, turn_codes.reshape(-1)))
    return turned.reshape(NR, NC, fields, P_SIZE, P_SIZE).transpose(2, 0, 3, 1, 4).reshape(fields, NR * P_SIZE, NC * P_SIZE)

def fold_back(running):
    middle = running[:, :, RIM:-RIM]
    middle = middle.at[:, :, :RIM].add(running[:, :, -RIM:])
    middle = middle.at[:, :, -RIM:].add(running[:, :, :RIM])
    interior = middle[:, RIM:-RIM]
    interior = interior.at[:, :RIM].add(middle[:, -RIM:])
    interior = interior.at[:, -RIM:].add(middle[:, :RIM])
    return interior

def evaluate(glob_field, cond_padded, orient, corner_points, w_state, w_cond, w_out, embedding, input_scale):
    fields = glob_field.shape[0]
    extent = P_SIZE + 2 * RIM
    padded = jnp.pad(glob_field, ((0, 0), (RIM, RIM), (RIM, RIM)), mode='wrap')

    def one_tile(running, tile_index):
        tile_row = tile_index // NC
        tile_col = tile_index % NC
        corner_cut = corner_flags(corner_points, tile_row, tile_col)
        keep_mask = corner_keep(corner_cut, P_SIZE)
        offsets = (jnp.zeros((), jnp.int32), (tile_row * P_SIZE).astype(jnp.int32), (tile_col * P_SIZE).astype(jnp.int32))
        window = lax.dynamic_slice(padded, offsets, (fields, extent, extent)) * keep_mask
        cond_window = lax.dynamic_slice(cond_padded, offsets, (fields, extent, extent)) * keep_mask
        turn_code = orient[tile_row, tile_col]
        own_cond = rotate_by(cond_window, turn_code).astype(jnp.bfloat16)
        feature = jnp.dot(w_cond, patches(own_cond), preferred_element_type=jnp.float32)
        guided = predict(rotate_by(window, turn_code), feature, w_state, w_out, embedding, input_scale)
        returned = rotate_by(guided, (4 - turn_code) % 4) * keep_mask
        current = lax.dynamic_slice(running, offsets, (fields, extent, extent))
        return (lax.dynamic_update_slice(running, current + returned, offsets), None)
    running = jnp.zeros((fields, ROWS + 2 * RIM, COLS + 2 * RIM), jnp.float32)
    running, unused = lax.scan(one_tile, running, jnp.arange(NR * NC, dtype=jnp.int32))
    total = fold_back(running)
    row_ids = jnp.arange(ROWS, dtype=jnp.int32)[:, None]
    col_ids = jnp.arange(COLS, dtype=jnp.int32)[None, :]
    corner_cut = corner_flags(corner_points, row_ids // P_SIZE, col_ids // P_SIZE)
    coverage = coverage_of(row_ids % P_SIZE, col_ids % P_SIZE, corner_cut, P_SIZE)
    return total / coverage[None]

def reference(noisy_state, conditioning, orient, corner_points, w_state, w_cond, w_out, embed_first, embed_second):
    to_global = (4 - orient) % 4
    glob_state = reframe(noisy_state, to_global)
    glob_cond = reframe(conditioning, to_global)
    cond_padded = jnp.pad(glob_cond, ((0, 0), (RIM, RIM), (RIM, RIM)), mode='wrap')
    slope_first = evaluate(glob_state, cond_padded, orient, corner_points, w_state, w_cond, w_out, embed_first, scale_first)
    middle = glob_state + step_size * slope_first
    slope_second = evaluate(middle, cond_padded, orient, corner_points, w_state, w_cond, w_out, embed_second, scale_second)
    updated = glob_state + 0.5 * step_size * (slope_first + slope_second)
    return reframe(updated, orient)
```

```python
import functools
import math

import jax
import jax.numpy as jnp
from jax import lax
from jax.experimental import pallas as pl
from jax.experimental.pallas import tpu as pltpu
from jax.sharding import PartitionSpec as P

RIM = 8
PAD = 16
MESH = pl.DeviceIdType.MESH

guide_weight = 2.0
sigma_first = 1.0
sigma_second = 0.6
step_size = sigma_second - sigma_first
scale_first = 1.0 / math.sqrt(1.0 + sigma_first**2)
scale_second = 1.0 / math.sqrt(1.0 + sigma_second**2)


def corner_flags(corner_points, tile_row, tile_col):
    grid_rows, grid_cols = corner_points.shape
    next_row = (tile_row + 1) % grid_rows
    next_col = (tile_col + 1) % grid_cols
    return (
        corner_points[tile_row, tile_col],
        corner_points[tile_row, next_col],
        corner_points[next_row, tile_col],
        corner_points[next_row, next_col],
    )


def turned(picture, code):
    picture = jnp.where(code % 2 == 1, jnp.swapaxes(picture, -1, -2), picture)
    picture = jnp.where((code == 1) | (code == 2), picture[..., ::-1, :], picture)
    return jnp.where(code >= 2, picture[..., ::-1], picture)


def lane_masks(corner_cuts, side, width):
    lane = jnp.arange(width, dtype=jnp.int32)
    masks = []
    for position, cut in enumerate(corner_cuts):
        col = (lane - (position * side - RIM)) % width
        valid = col < side + 2 * RIM
        left = col < RIM
        right = valid & (col >= side + RIM)
        top = valid & ~(left & (cut[0] == 1)) & ~(right & (cut[1] == 1))
        low = valid & ~(left & (cut[2] == 1)) & ~(right & (cut[3] == 1))
        masks.append(jnp.stack([top, valid, low]))
    return jnp.broadcast_to(
        jnp.stack(masks).astype(jnp.float32)[:, :, None, :], (len(corner_cuts), 3, PAD, width)
    )


def inverse_coverage(corner_cuts, side):
    local_col = jnp.arange(side, dtype=jnp.int32)
    left = local_col < RIM
    right = local_col >= side - RIM
    rows = []
    for kind in range(3):
        parts = []
        for cut in corner_cuts:
            cover = 1.0 + left.astype(jnp.float32) + right.astype(jnp.float32)
            if kind != 1:
                first, second = (cut[0], cut[1]) if kind == 0 else (cut[2], cut[3])
                cover = cover + 1.0
                cover = cover + (left & (first == 0)).astype(jnp.float32)
                cover = cover + (right & (second == 0)).astype(jnp.float32)
            parts.append(cover)
        rows.append(jnp.concatenate(parts))
    cover = jnp.stack(rows)
    return jnp.broadcast_to((1.0 / cover)[:, None, :], (3, PAD, cover.shape[1]))


def tap_variants(taps):
    return jnp.stack([jnp.rot90(taps, (4 - quarter) % 4, axes=(0, 1)) for quarter in range(4)])


def kernel(
    side,
    gs, gc, wm, wc, wo, e1, e2, msk, icov,
    out,
    exs, exc, exm, win, feat, prod, total, sl1,
    ps, pr, fr, fps, fpr,
    send, recv,
):
    width = gs.shape[2]
    extent = side + 2 * RIM
    blocks = extent // RIM
    tiles = wm.shape[0]
    n_tile = lax.axis_size("tile")
    n_face = lax.axis_size("face")
    my_tile = lax.axis_index("tile")
    my_face = lax.axis_index("face")

    def device(d_tile, d_face):
        return {
            "tile": lax.rem(my_tile + d_tile + n_tile, n_tile),
            "face": lax.rem(my_face + d_face + n_face, n_face),
        }

    around = [(dt, df) for dt in (-1, 0, 1) for df in (-1, 0, 1) if (dt, df) != (0, 0)]
    barrier = pltpu.get_barrier_semaphore()
    for dt, df in around:
        pl.semaphore_signal(barrier, inc=1, device_id=device(dt, df), device_id_type=MESH)
    pl.semaphore_wait(barrier, len(around))

    lane = lax.broadcasted_iota(jnp.int32, (PAD, width), 1)
    slots = (blocks + 2) // 2

    def remote(src, dst, phase, number, dt, df):
        return pltpu.make_async_remote_copy(
            src_ref=src,
            dst_ref=dst,
            send_sem=send.at[phase, number],
            recv_sem=recv.at[phase, number],
            device_id=device(dt, df),
            device_id_type=MESH,
        )

    def packed(load, shift, first):
        value = jnp.zeros((PAD, width), jnp.float32)
        for k in range(RIM):
            place = k + first
            moved = pltpu.roll(load(k), lax.rem(shift + RIM * place, width), 1)
            value = jnp.where(lane // RIM == place, moved, value)
        return value

    def unpacked(slot, shift, place):
        return pltpu.roll(slot, lax.rem(2 * width - shift - RIM * place, width), 1)

    def kind_of(block, low, high):
        return jnp.where(block == low, 0, jnp.where(block == high, 2, 1))

    def start_exchange(ex, phase, buf):
        def pack_block(block, _):
            slot = (block + 1) // 2
            first = RIM * lax.rem(block + 1, 2)
            for group in range(2):
                part = packed(lambda k: ex[block * RIM + k], RIM * group, first)
                ps[buf, group, slot] = ps[buf, group, slot] + part
            return 0

        ps[buf] = jnp.zeros(ps.shape[1:], jnp.float32)
        lax.fori_loop(1, blocks - 1, pack_block, 0)
        copies = [
            remote(ex.at[pl.ds(RIM, RIM)], ex.at[pl.ds(side + RIM, RIM)], phase, 0, 0, -1),
            remote(ex.at[pl.ds(side, RIM)], ex.at[pl.ds(0, RIM)], phase, 1, 0, 1),
        ]
        for group, dt in ((0, -1), (1, 1)):
            base = 2 + 3 * group
            mid = pl.ds(1, slots - 2)
            copies += [
                remote(ps.at[buf, group, mid], pr.at[buf, group, mid], phase, base, dt, 0),
                remote(
                    ps.at[buf, group, 1], pr.at[buf, group, slots - 1], phase, base + 1, dt, -1
                ),
                remote(
                    ps.at[buf, group, slots - 2], pr.at[buf, group, 0], phase, base + 2, dt, 1
                ),
            ]
        for copy in copies:
            copy.start()
        return copies

    def finish(copies):
        for copy in copies:
            copy.wait()

    def windows(ex, buf, scale):
        for p in range(tiles):
            for b in range(3):
                win[p, b, 0] = jnp.zeros((PAD, width), jnp.bfloat16)
                win[p, b, extent + 1] = jnp.zeros((PAD, width), jnp.bfloat16)

        def window_block(block, _):
            kind = kind_of(block, 0, blocks - 1)
            slot = (block + 1) // 2
            first = RIM * lax.rem(block + 1, 2)
            after = pr[buf, 0, slot]
            before = pr[buf, 1, slot]
            for k in range(RIM):
                row = block * RIM + k
                body = ex[row]
                left = jnp.where(lane >= width - RIM, unpacked(before, RIM, first + k), body)
                right = jnp.where(lane < RIM, unpacked(after, 0, first + k), body)
                for p, picture in ((0, left), (1, right)):
                    value = jnp.where(msk[p, kind] > 0, scale * picture, 0.0)
                    win[p, 0, row + 1] = pltpu.roll(value, 1, 1).astype(jnp.bfloat16)
                    win[p, 1, row + 1] = value.astype(jnp.bfloat16)
                    win[p, 2, row + 1] = pltpu.roll(value, width - 1, 1).astype(jnp.bfloat16)
            return 0

        lax.fori_loop(0, blocks, window_block, 0)

    def patch(p, first_row):
        taps = []
        for a in range(3):
            for b in range(3):
                rows = win[p, b, pl.ds(first_row + a, RIM)]
                taps.append(jnp.concatenate([rows[r] for r in range(RIM)], axis=1))
        return jnp.concatenate(taps, axis=0)

    def features():
        def feature_block(step, _):
            p = step // blocks
            block = lax.rem(step, blocks)
            feat[p, block] = jnp.dot(
                wc[p], patch(p, block * RIM), preferred_element_type=jnp.float32
            )
            return 0

        lax.fori_loop(0, tiles * blocks, feature_block, 0)

    def predictions(embedding):
        def predict_block(step, _):
            p = step // blocks
            block = lax.rem(step, blocks)
            mixed = jnp.dot(wm[p], patch(p, block * RIM), preferred_element_type=jnp.float32)
            mixed = mixed + embedding[...]
            cond = mixed + feat[p, block]
            plain_hidden = (mixed + mixed * jnp.tanh(mixed)).astype(jnp.bfloat16)
            cond_hidden = (cond + cond * jnp.tanh(cond)).astype(jnp.bfloat16)
            both = jnp.concatenate([cond_hidden, plain_hidden], axis=0)
            z = jnp.dot(wo[p], both, preferred_element_type=jnp.float32)
            for r in range(RIM):
                prod[p, block * RIM + 1 + r] = z[:, r * width : (r + 1) * width]
            return 0

        lax.fori_loop(0, tiles * blocks, predict_block, 0)

    def start_fold(phase, buf):
        fps[buf] = jnp.zeros(fps.shape[1:], jnp.float32)

        def spread_block(block, _):
            kind = kind_of(block, 0, blocks - 1)
            slot = (block + 1) // 2
            first = RIM * lax.rem(block + 1, 2)
            halves = ([], [])
            for k in range(RIM):
                row = block * RIM + k
                outs = []
                for p in range(tiles):
                    acc = []
                    for b in range(3):
                        acc.append(
                            prod[p, row, pl.ds(PAD * b, PAD)]
                            + prod[p, row + 1, pl.ds(PAD * (3 + b), PAD)]
                            + prod[p, row + 2, pl.ds(PAD * (6 + b), PAD)]
                        )
                    valid = msk[p, 1]
                    summed = (
                        acc[1]
                        + pltpu.roll(acc[0] * valid, 1, 1)
                        + pltpu.roll(acc[2] * valid, width - 1, 1)
                    )
                    outs.append(summed * msk[p, kind])
                total[buf, row] = jnp.where(lane < 3 * width // 4, outs[0], 0.0) + jnp.where(
                    lane >= width // 4, outs[1], 0.0
                )
                halves[0].append(outs[1])
                halves[1].append(outs[0])
            for group in range(2):
                part = packed(lambda k: halves[group][k], RIM * group, first)
                fps[buf, group, slot] = fps[buf, group, slot] + part
            return 0

        lax.fori_loop(0, blocks, spread_block, 0)
        copies = [
            remote(total.at[buf, pl.ds(0, RIM)], fr.at[buf, 1], phase, 0, 0, -1),
            remote(total.at[buf, pl.ds(side + RIM, RIM)], fr.at[buf, 0], phase, 1, 0, 1),
        ]
        for group, dt in ((0, 1), (1, -1)):
            base = 2 + 3 * group
            mid = pl.ds(1, slots - 2)
            copies += [
                remote(fps.at[buf, group, mid], fpr.at[buf, group, mid], phase, base, dt, 0),
                remote(fps.at[buf, group, 0], fpr.at[buf, group, 0], phase, base + 1, dt, -1),
                remote(
                    fps.at[buf, group, slots - 1],
                    fpr.at[buf, group, slots - 1],
                    phase,
                    base + 2,
                    dt,
                    1,
                ),
            ]
        for copy in copies:
            copy.start()
        return copies

    def fold(buf, use):
        for group in range(2):
            fpr[buf, group, slots - 2] = fpr[buf, group, slots - 2] + fpr[buf, group, 0]
            fpr[buf, group, 1] = fpr[buf, group, 1] + fpr[buf, group, slots - 1]
        total[buf, pl.ds(RIM, RIM)] = total[buf, pl.ds(RIM, RIM)] + fr[buf, 0]
        total[buf, pl.ds(side, RIM)] = total[buf, pl.ds(side, RIM)] + fr[buf, 1]

        def fold_block(block, _):
            kind = kind_of(block, 1, blocks - 2)
            slot = (block + 1) // 2
            first = RIM * lax.rem(block + 1, 2)
            low = fpr[buf, 0, slot]
            high = fpr[buf, 1, slot]
            scale = icov[kind]
            for k in range(RIM):
                row = block * RIM + k
                value = total[buf, row]
                value = value + jnp.where(lane < RIM, unpacked(low, 0, first + k), 0.0)
                value = value + jnp.where(
                    lane >= width - RIM, unpacked(high, RIM, first + k), 0.0
                )
                use(row, value * scale)
            return 0

        lax.fori_loop(1, blocks - 1, fold_block, 0)

    exc[pl.ds(RIM, side)] = gc[...]
    cond_copies = start_exchange(exc, 0, 0)
    exs[pl.ds(RIM, side)] = gs[...]
    state_copies = start_exchange(exs, 1, 1)
    for p in range(tiles):
        prod[p, 0] = jnp.zeros(prod.shape[2:], jnp.float32)
        prod[p, extent + 1] = jnp.zeros(prod.shape[2:], jnp.float32)
    finish(cond_copies)
    windows(exc, 0, 1.0)
    features()
    finish(state_copies)
    windows(exs, 1, scale_first)
    predictions(e1)
    copies = start_fold(2, 0)
    finish(copies)

    def first_use(row, slope):
        sl1[row - RIM] = slope
        exm[row] = gs[row - RIM] + step_size * slope

    fold(0, first_use)
    copies = start_exchange(exm, 3, 2)
    finish(copies)
    windows(exm, 2, scale_second)
    predictions(e2)
    copies = start_fold(4, 1)
    finish(copies)

    def second_use(row, slope):
        out[row - RIM] = gs[row - RIM] + 0.5 * step_size * (sl1[row - RIM] + slope)

    fold(1, second_use)


def local(
    noisy_state,
    conditioning,
    orient,
    corner_points,
    w_state,
    w_cond,
    w_out,
    embed_first,
    embed_second,
):
    fields, side, width = noisy_state.shape
    tiles = width // side
    extent = side + 2 * RIM
    hidden = w_state.shape[0]
    tile_row = lax.axis_index("face")
    col_base = lax.axis_index("tile") * tiles
    codes = lax.dynamic_slice(orient, (tile_row, col_base), (1, tiles))[0]

    def into_rows(field):
        parts = [
            turned(field[:, :, p * side : (p + 1) * side], (4 - codes[p]) % 4)
            for p in range(tiles)
        ]
        whole = jnp.transpose(jnp.concatenate(parts, axis=2), (1, 0, 2))
        return jnp.pad(whole, ((0, 0), (0, PAD - fields), (0, 0)))

    gs = into_rows(noisy_state)
    gc = into_rows(conditioning)

    def inner_weights(weights):
        taps = weights.reshape(hidden, 3, 3, fields).transpose(1, 2, 0, 3)
        variants = jnp.pad(tap_variants(taps), ((0, 0),) * 4 + ((0, PAD - fields),))
        variants = variants.transpose(0, 3, 1, 2, 4).reshape(4, hidden, 9 * PAD)
        return (0.5 * variants[codes]).astype(jnp.bfloat16)

    wm = inner_weights(w_state)
    wc = inner_weights(w_cond)
    taps = w_out.reshape(3, 3, fields, hidden)
    variants = jnp.pad(
        tap_variants(taps), ((0, 0), (0, 0), (0, 0), (0, PAD - fields), (0, 0))
    ).reshape(4, 9 * PAD, hidden)[codes]
    wo = jnp.concatenate([guide_weight * variants, (1.0 - guide_weight) * variants], axis=2)
    wo = wo.astype(jnp.bfloat16)
    spread_lanes = (hidden, RIM * width)
    e1 = jnp.broadcast_to(0.5 * embed_first[:, None], spread_lanes)
    e2 = jnp.broadcast_to(0.5 * embed_second[:, None], spread_lanes)
    cuts = [corner_flags(corner_points, tile_row, col_base + p) for p in range(tiles)]
    msk = lane_masks(cuts, side, width)
    icov = inverse_coverage(cuts, side)

    slots = (extent // RIM + 2) // 2
    f32 = jnp.float32
    vmem = pl.BlockSpec(memory_space=pltpu.VMEM)
    updated = pl.pallas_call(
        functools.partial(kernel, side),
        out_shape=jax.ShapeDtypeStruct((side, PAD, width), f32),
        in_specs=[vmem] * 9,
        out_specs=vmem,
        scratch_shapes=[
            pltpu.VMEM((extent, PAD, width), f32),
            pltpu.VMEM((extent, PAD, width), f32),
            pltpu.VMEM((extent, PAD, width), f32),
            pltpu.VMEM((tiles, 3, extent + 2, PAD, width), jnp.bfloat16),
            pltpu.VMEM((tiles, extent // RIM, hidden, RIM * width), f32),
            pltpu.VMEM((tiles, extent + 2, 9 * PAD, width), f32),
            pltpu.VMEM((2, extent, PAD, width), f32),
            pltpu.VMEM((side, PAD, width), f32),
            pltpu.VMEM((3, 2, slots, PAD, width), f32),
            pltpu.VMEM((3, 2, slots, PAD, width), f32),
            pltpu.VMEM((2, 2, RIM, PAD, width), f32),
            pltpu.VMEM((2, 2, slots, PAD, width), f32),
            pltpu.VMEM((2, 2, slots, PAD, width), f32),
            pltpu.SemaphoreType.DMA((5, 8)),
            pltpu.SemaphoreType.DMA((5, 8)),
        ],
        compiler_params=pltpu.CompilerParams(
            collective_id=0, has_side_effects=True, vmem_limit_bytes=50 * 1024 * 1024
        ),
    )(gs, gc, wm, wc, wo, e1, e2, msk, icov)

    updated = jnp.transpose(updated[:, :fields], (1, 0, 2))
    return jnp.concatenate(
        [turned(updated[:, :, p * side : (p + 1) * side], codes[p]) for p in range(tiles)],
        axis=2,
    )


def solution(mesh):
    return jax.shard_map(
        local,
        mesh=mesh,
        in_specs=(
            P("groups", "face", "tile"),
            P("groups", "face", "tile"),
            P(),
            P(),
            P(),
            P(),
            P(),
            P(),
            P(),
        ),
        out_specs=P("groups", "face", "tile"),
        check_vma=False,
    )
```

```python
import functools
import math

import jax
import jax.numpy as jnp
from jax import lax
from jax.experimental import pallas as pl
from jax.experimental.pallas import tpu as pltpu
from jax.sharding import PartitionSpec as P

RIM = 8
PAD = 16
MESH = pl.DeviceIdType.MESH

guide_weight = 2.0
sigma_first = 1.0
sigma_second = 0.6
step_size = sigma_second - sigma_first
scale_first = 1.0 / math.sqrt(1.0 + sigma_first**2)
scale_second = 1.0 / math.sqrt(1.0 + sigma_second**2)


def kernel(
    side,
    noisy, given, orient, corners, ws_t, wc_t, w_out, e1, e2,
    out,
    wm, wc, wo, emb, msk, icov, turned_rows, updated,
    exs, exc, exm, win, feat, prod, total, sl1,
    ps, pr, fr, fps, fpr,
    send, recv,
):
    fields, _, width = noisy.shape
    hidden = w_out.shape[1]
    extent = side + 2 * RIM
    blocks = extent // RIM
    tiles = width // side
    n_tile = lax.axis_size("tile")
    n_face = lax.axis_size("face")
    my_tile = lax.axis_index("tile")
    my_face = lax.axis_index("face")

    def device(d_tile, d_face):
        return {
            "tile": lax.rem(my_tile + d_tile + n_tile, n_tile),
            "face": lax.rem(my_face + d_face + n_face, n_face),
        }

    around = [(dt, df) for dt in (-1, 0, 1) for df in (-1, 0, 1) if (dt, df) != (0, 0)]
    barrier = pltpu.get_barrier_semaphore()
    for dt, df in around:
        pl.semaphore_signal(barrier, inc=1, device_id=device(dt, df), device_id_type=MESH)
    pl.semaphore_wait(barrier, len(around))

    lane = lax.broadcasted_iota(jnp.int32, (PAD, width), 1)
    slots = (blocks + 2) // 2

    def remote(src, dst, phase, number, dt, df):
        return pltpu.make_async_remote_copy(
            src_ref=src,
            dst_ref=dst,
            send_sem=send.at[phase, number],
            recv_sem=recv.at[phase, number],
            device_id=device(dt, df),
            device_id_type=MESH,
        )

    def packed(load, shift, first):
        value = jnp.zeros((PAD, width), jnp.float32)
        for k in range(RIM):
            place = k + first
            moved = pltpu.roll(load(k), lax.rem(shift + RIM * place, width), 1)
            value = jnp.where(lane // RIM == place, moved, value)
        return value

    def unpacked(slot, shift, place):
        return pltpu.roll(slot, lax.rem(2 * width - shift - RIM * place, width), 1)

    def kind_of(block, low, high):
        return jnp.where(block == low, 0, jnp.where(block == high, 2, 1))

    def start_exchange(ex, phase, buf):
        def pack_block(block, _):
            slot = (block + 1) // 2
            first = RIM * lax.rem(block + 1, 2)
            for group in range(2):
                part = packed(lambda k: ex[block * RIM + k], RIM * group, first)
                ps[buf, group, slot] = ps[buf, group, slot] + part
            return 0

        ps[buf] = jnp.zeros(ps.shape[1:], jnp.float32)
        lax.fori_loop(1, blocks - 1, pack_block, 0)
        copies = [
            remote(ex.at[pl.ds(RIM, RIM)], ex.at[pl.ds(side + RIM, RIM)], phase, 0, 0, -1),
            remote(ex.at[pl.ds(side, RIM)], ex.at[pl.ds(0, RIM)], phase, 1, 0, 1),
        ]
        for group, dt in ((0, -1), (1, 1)):
            base = 2 + 3 * group
            mid = pl.ds(1, slots - 2)
            copies += [
                remote(ps.at[buf, group, mid], pr.at[buf, group, mid], phase, base, dt, 0),
                remote(
                    ps.at[buf, group, 1], pr.at[buf, group, slots - 1], phase, base + 1, dt, -1
                ),
                remote(
                    ps.at[buf, group, slots - 2], pr.at[buf, group, 0], phase, base + 2, dt, 1
                ),
            ]
        for copy in copies:
            copy.start()
        return copies

    def finish(copies):
        for copy in copies:
            copy.wait()

    def windows(ex, buf, scale):
        for p in range(tiles):
            for b in range(3):
                win[p, b, 0] = jnp.zeros((PAD, width), jnp.bfloat16)
                win[p, b, extent + 1] = jnp.zeros((PAD, width), jnp.bfloat16)

        def window_block(block, _):
            kind = kind_of(block, 0, blocks - 1)
            slot = (block + 1) // 2
            first = RIM * lax.rem(block + 1, 2)
            after = pr[buf, 0, slot]
            before = pr[buf, 1, slot]
            for k in range(RIM):
                row = block * RIM + k
                body = ex[row]
                left = jnp.where(lane >= width - RIM, unpacked(before, RIM, first + k), body)
                right = jnp.where(lane < RIM, unpacked(after, 0, first + k), body)
                for p, picture in ((0, left), (1, right)):
                    value = jnp.where(msk[p, kind] > 0, scale * picture, 0.0)
                    win[p, 0, row + 1] = pltpu.roll(value, 1, 1).astype(jnp.bfloat16)
                    win[p, 1, row + 1] = value.astype(jnp.bfloat16)
                    win[p, 2, row + 1] = pltpu.roll(value, width - 1, 1).astype(jnp.bfloat16)
            return 0

        lax.fori_loop(0, blocks, window_block, 0)

    def patch(p, first_row):
        taps = []
        for a in range(3):
            for b in range(3):
                rows = win[p, b, pl.ds(first_row + a, RIM)]
                taps.append(jnp.concatenate([rows[r] for r in range(RIM)], axis=1))
        return jnp.concatenate(taps, axis=0)

    def features():
        def feature_block(step, _):
            p = step // blocks
            block = lax.rem(step, blocks)
            feat[p, block] = jnp.dot(
                wc[p], patch(p, block * RIM), preferred_element_type=jnp.float32
            )
            return 0

        lax.fori_loop(0, tiles * blocks, feature_block, 0)

    def predictions(number):
        def predict_block(step, _):
            p = step // blocks
            block = lax.rem(step, blocks)
            mixed = jnp.dot(wm[p], patch(p, block * RIM), preferred_element_type=jnp.float32)
            mixed = mixed + jnp.concatenate([emb[number]] * RIM, axis=1)
            cond = mixed + feat[p, block]
            plain_hidden = (mixed + mixed * jnp.tanh(mixed)).astype(jnp.bfloat16)
            cond_hidden = (cond + cond * jnp.tanh(cond)).astype(jnp.bfloat16)
            both = jnp.concatenate([cond_hidden, plain_hidden], axis=0)
            z = jnp.dot(wo[p], both, preferred_element_type=jnp.float32)
            for r in range(RIM):
                prod[p, block * RIM + 1 + r] = z[:, r * width : (r + 1) * width]
            return 0

        lax.fori_loop(0, tiles * blocks, predict_block, 0)

    def start_fold(phase, buf):
        fps[buf] = jnp.zeros(fps.shape[1:], jnp.float32)

        def spread_block(block, _):
            kind = kind_of(block, 0, blocks - 1)
            slot = (block + 1) // 2
            first = RIM * lax.rem(block + 1, 2)
            halves = ([], [])
            for k in range(RIM):
                row = block * RIM + k
                outs = []
                for p in range(tiles):
                    acc = []
                    for b in range(3):
                        acc.append(
                            prod[p, row, pl.ds(PAD * b, PAD)]
                            + prod[p, row + 1, pl.ds(PAD * (3 + b), PAD)]
                            + prod[p, row + 2, pl.ds(PAD * (6 + b), PAD)]
                        )
                    valid = msk[p, 1]
                    summed = (
                        acc[1]
                        + pltpu.roll(acc[0] * valid, 1, 1)
                        + pltpu.roll(acc[2] * valid, width - 1, 1)
                    )
                    outs.append(summed * msk[p, kind])
                total[buf, row] = jnp.where(lane < 3 * width // 4, outs[0], 0.0) + jnp.where(
                    lane >= width // 4, outs[1], 0.0
                )
                halves[0].append(outs[1])
                halves[1].append(outs[0])
            for group in range(2):
                part = packed(lambda k: halves[group][k], RIM * group, first)
                fps[buf, group, slot] = fps[buf, group, slot] + part
            return 0

        lax.fori_loop(0, blocks, spread_block, 0)
        copies = [
            remote(total.at[buf, pl.ds(0, RIM)], fr.at[buf, 1], phase, 0, 0, -1),
            remote(total.at[buf, pl.ds(side + RIM, RIM)], fr.at[buf, 0], phase, 1, 0, 1),
        ]
        for group, dt in ((0, 1), (1, -1)):
            base = 2 + 3 * group
            mid = pl.ds(1, slots - 2)
            copies += [
                remote(fps.at[buf, group, mid], fpr.at[buf, group, mid], phase, base, dt, 0),
                remote(fps.at[buf, group, 0], fpr.at[buf, group, 0], phase, base + 1, dt, -1),
                remote(
                    fps.at[buf, group, slots - 1],
                    fpr.at[buf, group, slots - 1],
                    phase,
                    base + 2,
                    dt,
                    1,
                ),
            ]
        for copy in copies:
            copy.start()
        return copies

    def fold(buf, use):
        for group in range(2):
            fpr[buf, group, slots - 2] = fpr[buf, group, slots - 2] + fpr[buf, group, 0]
            fpr[buf, group, 1] = fpr[buf, group, 1] + fpr[buf, group, slots - 1]
        total[buf, pl.ds(RIM, RIM)] = total[buf, pl.ds(RIM, RIM)] + fr[buf, 0]
        total[buf, pl.ds(side, RIM)] = total[buf, pl.ds(side, RIM)] + fr[buf, 1]

        def fold_block(block, _):
            kind = kind_of(block, 1, blocks - 2)
            slot = (block + 1) // 2
            first = RIM * lax.rem(block + 1, 2)
            low = fpr[buf, 0, slot]
            high = fpr[buf, 1, slot]
            scale = icov[kind]
            for k in range(RIM):
                row = block * RIM + k
                value = total[buf, row]
                value = value + jnp.where(lane < RIM, unpacked(low, 0, first + k), 0.0)
                value = value + jnp.where(
                    lane >= width - RIM, unpacked(high, RIM, first + k), 0.0
                )
                use(row, value * scale)
            return 0

        lax.fori_loop(1, blocks - 1, fold_block, 0)

    codes = [orient[my_face, my_tile * tiles + p] for p in range(tiles)]

    def per_lane(values, shape):
        return jnp.where(lax.broadcasted_iota(jnp.int32, shape, 1) < side, values[0], values[1])

    def flips_columns(code):
        return (code == 1) | (code == 2)

    picture_codes = per_lane(codes, (side, width))
    transposes = lax.rem(picture_codes, 2) == 1
    source_lane = lax.broadcasted_iota(jnp.int32, (width, width), 0)
    target_lane = lax.broadcasted_iota(jnp.int32, (width, width), 1)
    tile_start = jnp.where(target_lane < side, 0, side)
    mirrored = 2 * tile_start + side - 1 - target_lane
    wanted = jnp.where(flips_columns(per_lane(codes, (width, width))), mirrored, target_lane)
    swap = jnp.where(source_lane == wanted, 1.0, 0.0).astype(jnp.bfloat16)
    swap = jnp.concatenate([swap, swap, swap], axis=0)

    def flipped(value):
        first = value.astype(jnp.bfloat16)
        rest = value - first.astype(jnp.float32)
        second = rest.astype(jnp.bfloat16)
        third = (rest - second.astype(jnp.float32)).astype(jnp.bfloat16)
        parts = jnp.concatenate([first, second, third], axis=1)
        return jnp.dot(parts, swap, preferred_element_type=jnp.float32)

    def transposed(picture):
        other = jnp.transpose(picture)
        other = jnp.concatenate([other[:side], other[side:]], axis=1)
        return jnp.where(transposes, other, picture)

    def source_row(p, row):
        return jnp.where(codes[p] >= 2, side - 1 - row, row)

    turned_rows[...] = jnp.zeros(turned_rows.shape, jnp.float32)

    def into_rows(field, ex):
        for channel in range(fields):
            picture = flipped(transposed(field[channel]))
            turned_rows[pl.ds(channel, side, stride=PAD)] = picture

        def one_row(row, _):
            first = turned_rows[pl.ds(PAD * source_row(0, row), PAD)]
            second = turned_rows[pl.ds(PAD * source_row(1, row), PAD)]
            ex[row + RIM] = jnp.where(lane < side, first, second)
            return 0

        lax.fori_loop(0, side, one_row, 0)

    into_rows(given, exc)
    cond_copies = start_exchange(exc, 0, 0)
    into_rows(noisy, exs)
    state_copies = start_exchange(exs, 1, 1)
    grid_rows, grid_cols = corners.shape
    next_row = lax.rem(my_face + 1, grid_rows)
    cover_rows = []
    for p in range(tiles):
        here = my_tile * tiles + p
        beside = lax.rem(here + 1, grid_cols)
        cuts = [
            corners[my_face, here],
            corners[my_face, beside],
            corners[next_row, here],
            corners[next_row, beside],
        ]
        col = lax.rem(lane + width - (p * side - RIM), width)
        ones = jnp.where(col < extent, 1.0, 0.0)
        left = col < RIM
        right = (col >= side + RIM) & (col < extent)
        cut_low, cut_high = [
            jnp.where(left, cuts[k], jnp.where(right, cuts[k + 1], 0)) for k in (0, 2)
        ]
        msk[p, 0] = jnp.where(cut_low == 1, 0.0, ones)
        msk[p, 1] = ones
        msk[p, 2] = jnp.where(cut_high == 1, 0.0, ones)
        inner = lane - p * side
        left = inner < RIM
        right = inner >= side - RIM
        band = jnp.where(left | right, 1.0, 0.0)
        cut_low, cut_high = [
            jnp.where(left, cuts[k], jnp.where(right, cuts[k + 1], 1)) for k in (0, 2)
        ]
        cover_rows.append(
            (
                2.0 + band + jnp.where(cut_low == 1, 0.0, 1.0),
                1.0 + band,
                2.0 + band + jnp.where(cut_high == 1, 0.0, 1.0),
            )
        )
        tap_col = lax.broadcasted_iota(jnp.int32, (9 * PAD, 9 * fields), 0)
        tap = tap_col // PAD
        channel = tap_col - tap * PAD
        a = jnp.where(tap >= 6, 2, jnp.where(tap >= 3, 1, 0))
        b = tap - 3 * a
        code = codes[p]
        source_a = jnp.where(
            code == 0, a, jnp.where(code == 3, b, jnp.where(code == 2, 2 - a, 2 - b))
        )
        source_b = jnp.where(
            code == 0, b, jnp.where(code == 3, 2 - a, jnp.where(code == 2, 2 - b, a))
        )
        source = (3 * source_a + source_b) * fields + channel
        place = lax.broadcasted_iota(jnp.int32, (9 * PAD, 9 * fields), 1)
        pick = jnp.where((source == place) & (channel < fields), 1.0, 0.0).astype(jnp.bfloat16)
        for weights, inner_weights in ((wm, ws_t), (wc, wc_t)):
            taps = jnp.dot(pick, inner_weights[...], preferred_element_type=jnp.float32)
            weights[p] = (0.5 * jnp.transpose(taps)).astype(jnp.bfloat16)
        taps = jnp.dot(pick, w_out[...], preferred_element_type=jnp.float32)
        wo[p] = jnp.concatenate(
            [guide_weight * taps, (1.0 - guide_weight) * taps], axis=1
        ).astype(jnp.bfloat16)
    for kind in range(3):
        cover = jnp.where(lane < side, cover_rows[0][kind], cover_rows[1][kind])
        icov[kind] = 1.0 / cover
    for number, embedding in enumerate((e1, e2)):
        spread_out = jnp.broadcast_to(0.5 * embedding[...], (width, hidden))
        emb[number] = jnp.transpose(spread_out)
    for p in range(tiles):
        prod[p, 0] = jnp.zeros(prod.shape[2:], jnp.float32)
        prod[p, extent + 1] = jnp.zeros(prod.shape[2:], jnp.float32)
    finish(cond_copies)
    windows(exc, 0, 1.0)
    features()
    finish(state_copies)
    windows(exs, 1, scale_first)
    predictions(0)
    copies = start_fold(2, 0)
    finish(copies)

    def first_use(row, slope):
        sl1[row - RIM] = slope
        exm[row] = exs[row] + step_size * slope

    fold(0, first_use)
    copies = start_exchange(exm, 3, 2)
    finish(copies)
    windows(exm, 2, scale_second)
    predictions(1)
    copies = start_fold(4, 1)
    finish(copies)

    def second_use(row, slope):
        updated[row - RIM] = exs[row] + 0.5 * step_size * (sl1[row - RIM] + slope)

    fold(1, second_use)

    def turn_block(block, _):
        rows = []
        for k in range(RIM):
            row = block * RIM + k
            first = updated[source_row(0, row)]
            second = updated[source_row(1, row)]
            rows.append(jnp.where(lane < side, first, second))
        start = pl.multiple_of(block * RIM * PAD, RIM * PAD)
        turned_rows[pl.ds(start, RIM * PAD)] = flipped(jnp.concatenate(rows, axis=0))
        return 0

    lax.fori_loop(0, side // RIM, turn_block, 0)
    for channel in range(fields):
        out[channel] = transposed(turned_rows[pl.ds(channel, side, stride=PAD)])


def local(
    noisy_state,
    conditioning,
    orient,
    corner_points,
    w_state,
    w_cond,
    w_out,
    embed_first,
    embed_second,
):
    fields, side, width = noisy_state.shape
    tiles = width // side
    extent = side + 2 * RIM
    hidden = w_state.shape[0]
    slots = (extent // RIM + 2) // 2
    f32 = jnp.float32
    vmem = pl.BlockSpec(memory_space=pltpu.VMEM)
    smem = pl.BlockSpec(memory_space=pltpu.SMEM)
    return pl.pallas_call(
        functools.partial(kernel, side),
        out_shape=jax.ShapeDtypeStruct((fields, side, width), f32),
        in_specs=[vmem, vmem, smem, smem] + [vmem] * 5,
        out_specs=vmem,
        scratch_shapes=[
            pltpu.VMEM((tiles, hidden, 9 * PAD), jnp.bfloat16),
            pltpu.VMEM((tiles, hidden, 9 * PAD), jnp.bfloat16),
            pltpu.VMEM((tiles, 9 * PAD, 2 * hidden), jnp.bfloat16),
            pltpu.VMEM((2, hidden, width), f32),
            pltpu.VMEM((tiles, 3, PAD, width), f32),
            pltpu.VMEM((3, PAD, width), f32),
            pltpu.VMEM((side * PAD, width), f32),
            pltpu.VMEM((side, PAD, width), f32),
            pltpu.VMEM((extent, PAD, width), f32),
            pltpu.VMEM((extent, PAD, width), f32),
            pltpu.VMEM((extent, PAD, width), f32),
            pltpu.VMEM((tiles, 3, extent + 2, PAD, width), jnp.bfloat16),
            pltpu.VMEM((tiles, extent // RIM, hidden, RIM * width), f32),
            pltpu.VMEM((tiles, extent + 2, 9 * PAD, width), f32),
            pltpu.VMEM((2, extent, PAD, width), f32),
            pltpu.VMEM((side, PAD, width), f32),
            pltpu.VMEM((3, 2, slots, PAD, width), f32),
            pltpu.VMEM((3, 2, slots, PAD, width), f32),
            pltpu.VMEM((2, 2, RIM, PAD, width), f32),
            pltpu.VMEM((2, 2, slots, PAD, width), f32),
            pltpu.VMEM((2, 2, slots, PAD, width), f32),
            pltpu.SemaphoreType.DMA((5, 8)),
            pltpu.SemaphoreType.DMA((5, 8)),
        ],
        compiler_params=pltpu.CompilerParams(
            collective_id=0, has_side_effects=True, vmem_limit_bytes=50 * 1024 * 1024
        ),
    )(
        noisy_state,
        conditioning,
        orient,
        corner_points,
        w_state.T,
        w_cond.T,
        w_out,
        embed_first[None],
        embed_second[None],
    )


def solution(mesh):
    return jax.shard_map(
        local,
        mesh=mesh,
        in_specs=(
            P("groups", "face", "tile"),
            P("groups", "face", "tile"),
            P(),
            P(),
            P(),
            P(),
            P(),
            P(),
            P(),
        ),
        out_specs=P("groups", "face", "tile"),
        check_vma=False,
    )
```

```python
import functools
import math

import jax
import jax.numpy as jnp
from jax import lax
from jax.experimental import pallas as pl
from jax.experimental.pallas import tpu as pltpu
from jax.sharding import PartitionSpec as P

RIM = 8
PAD = 16
MESH = pl.DeviceIdType.MESH

guide_weight = 2.0
sigma_first = 1.0
sigma_second = 0.6
step_size = sigma_second - sigma_first
scale_first = 1.0 / math.sqrt(1.0 + sigma_first**2)
scale_second = 1.0 / math.sqrt(1.0 + sigma_second**2)


def kernel(
    side,
    noisy, given, orient, corners, ws_t, wc_t, w_out, e1, e2,
    out,
    wm, wc, wo, emb, msk, icov, turned_rows, updated,
    exs, exc, exm, win, feat, outs, total, sl1,
    ps, pr, fr, fps, fpr,
    send, recv,
):
    fields, _, width = noisy.shape
    hidden = w_out.shape[1]
    extent = side + 2 * RIM
    blocks = extent // RIM
    tiles = width // side
    n_tile = lax.axis_size("tile")
    n_face = lax.axis_size("face")
    my_tile = lax.axis_index("tile")
    my_face = lax.axis_index("face")

    def device(d_tile, d_face):
        return {
            "tile": lax.rem(my_tile + d_tile + n_tile, n_tile),
            "face": lax.rem(my_face + d_face + n_face, n_face),
        }

    around = [(dt, df) for dt in (-1, 0, 1) for df in (-1, 0, 1) if (dt, df) != (0, 0)]
    barrier = pltpu.get_barrier_semaphore()
    for dt, df in around:
        pl.semaphore_signal(barrier, inc=1, device_id=device(dt, df), device_id_type=MESH)
    pl.semaphore_wait(barrier, len(around))

    lane = lax.broadcasted_iota(jnp.int32, (PAD, width), 1)
    slots = (blocks + 2) // 2

    def remote(src, dst, phase, number, dt, df):
        return pltpu.make_async_remote_copy(
            src_ref=src,
            dst_ref=dst,
            send_sem=send.at[phase, number],
            recv_sem=recv.at[phase, number],
            device_id=device(dt, df),
            device_id_type=MESH,
        )

    def packed(load, shift, first):
        value = jnp.zeros((PAD, width), jnp.float32)
        for k in range(RIM):
            place = k + first
            moved = pltpu.roll(load(k), (shift + RIM * place) % width, 1)
            value = jnp.where(lane // RIM == place, moved, value)
        return value

    def unpacked(slot, shift, place):
        return pltpu.roll(slot, (-shift - RIM * place) % width, 1)

    def kind_of(block, low, high):
        return jnp.where(block == low, 0, jnp.where(block == high, 2, 1))

    def sweep(visit, ends):
        if ends:
            visit(0, 0, RIM, 0)

        def pair(slot, _):
            visit(2 * slot - 1, slot, 0, 1)
            visit(2 * slot, slot, RIM, 1)
            return 0

        lax.fori_loop(1, slots - 1, pair, 0)
        if ends:
            visit(blocks - 1, slots - 1, 0, 2)

    def start_exchange(ex, phase, buf):
        def pack_block(block, slot, first, _):
            for group in range(2):
                part = packed(lambda k: ex[block * RIM + k], RIM * group, first)
                ps[buf, group, slot] = ps[buf, group, slot] + part

        ps[buf] = jnp.zeros(ps.shape[1:], jnp.float32)
        sweep(pack_block, False)
        copies = [
            remote(ex.at[pl.ds(RIM, RIM)], ex.at[pl.ds(side + RIM, RIM)], phase, 0, 0, -1),
            remote(ex.at[pl.ds(side, RIM)], ex.at[pl.ds(0, RIM)], phase, 1, 0, 1),
        ]
        for group, dt in ((0, -1), (1, 1)):
            base = 2 + 3 * group
            mid = pl.ds(1, slots - 2)
            copies += [
                remote(ps.at[buf, group, mid], pr.at[buf, group, mid], phase, base, dt, 0),
                remote(
                    ps.at[buf, group, 1], pr.at[buf, group, slots - 1], phase, base + 1, dt, -1
                ),
                remote(
                    ps.at[buf, group, slots - 2], pr.at[buf, group, 0], phase, base + 2, dt, 1
                ),
            ]
        for copy in copies:
            copy.start()
        return copies

    def finish(copies):
        for copy in copies:
            copy.wait()

    def windows(ex, buf, scale):
        for p in range(tiles):
            for b in range(3):
                win[p, b, 0] = jnp.zeros((PAD, width), jnp.bfloat16)
                win[p, b, extent + 1] = jnp.zeros((PAD, width), jnp.bfloat16)

        def window_block(block, slot, first, kind):
            after = pr[buf, 0, slot]
            before = pr[buf, 1, slot]
            for k in range(RIM):
                row = block * RIM + k
                body = ex[row]
                left = jnp.where(lane >= width - RIM, unpacked(before, RIM, first + k), body)
                right = jnp.where(lane < RIM, unpacked(after, 0, first + k), body)
                for p, picture in ((0, left), (1, right)):
                    value = jnp.where(msk[p, kind] > 0, scale * picture, 0.0)
                    win[p, 0, row + 1] = pltpu.roll(value, 1, 1).astype(jnp.bfloat16)
                    win[p, 1, row + 1] = value.astype(jnp.bfloat16)
                    win[p, 2, row + 1] = pltpu.roll(value, width - 1, 1).astype(jnp.bfloat16)

        sweep(window_block, True)

    def patch(p, first_row):
        taps = []
        for a in range(3):
            for b in range(3):
                rows = win[p, b, pl.ds(first_row + a, RIM)]
                taps.append(jnp.concatenate([rows[r] for r in range(RIM)], axis=1))
        return jnp.concatenate(taps, axis=0)

    def features():
        def feature_block(step, _):
            p = step // blocks
            block = lax.rem(step, blocks)
            feat[p, block] = jnp.dot(
                wc[p], patch(p, block * RIM), preferred_element_type=jnp.float32
            )
            return 0

        lax.fori_loop(0, tiles * blocks, feature_block, 0)

    def predictions(number):
        group = 3 * PAD

        def finish_row(p, place, taps):
            valid = msk[p, 1]
            outs[p, place] = (
                taps[PAD : 2 * PAD]
                + pltpu.roll(taps[:PAD] * valid, 1, 1)
                + pltpu.roll(taps[2 * PAD :] * valid, width - 1, 1)
            )

        def predict_block(block, carry):
            later = []
            for p in range(tiles):
                pending, above = carry[p]
                mixed = jnp.dot(wm[p], patch(p, block * RIM), preferred_element_type=jnp.float32)
                mixed = mixed + jnp.concatenate([emb[number]] * RIM, axis=1)
                cond = mixed + feat[p, block]
                plain_hidden = (mixed + mixed * jnp.tanh(mixed)).astype(jnp.bfloat16)
                cond_hidden = (cond + cond * jnp.tanh(cond)).astype(jnp.bfloat16)
                both = jnp.concatenate([cond_hidden, plain_hidden], axis=0)
                z = jnp.dot(wo[p], both, preferred_element_type=jnp.float32)

                def part(a, r):
                    return z[a * group : (a + 1) * group, r * width : (r + 1) * width]

                start = block * RIM
                finish_row(p, start, pending + part(2, 0))
                finish_row(p, start + 1, above + part(1, 0) + part(2, 1))
                for r in range(1, RIM - 1):
                    finish_row(p, start + 1 + r, part(0, r - 1) + part(1, r) + part(2, r + 1))
                later.append((part(0, RIM - 2) + part(1, RIM - 1), part(0, RIM - 1)))
            return tuple(later)

        none = jnp.zeros((group, width), jnp.float32)
        carry = lax.fori_loop(0, blocks, predict_block, ((none, none),) * tiles)
        for p in range(tiles):
            finish_row(p, extent, carry[p][0])

    def start_fold(phase, buf):
        fps[buf] = jnp.zeros(fps.shape[1:], jnp.float32)

        def spread_block(block, slot, first, kind):
            halves = ([], [])
            for k in range(RIM):
                row = block * RIM + k
                first_out = outs[0, row + 1] * msk[0, kind]
                second_out = outs[1, row + 1] * msk[1, kind]
                total[buf, row] = jnp.where(lane < 3 * width // 4, first_out, 0.0) + jnp.where(
                    lane >= width // 4, second_out, 0.0
                )
                halves[0].append(second_out)
                halves[1].append(first_out)
            for group in range(2):
                part = packed(lambda k: halves[group][k], RIM * group, first)
                fps[buf, group, slot] = fps[buf, group, slot] + part

        sweep(spread_block, True)
        copies = [
            remote(total.at[buf, pl.ds(0, RIM)], fr.at[buf, 1], phase, 0, 0, -1),
            remote(total.at[buf, pl.ds(side + RIM, RIM)], fr.at[buf, 0], phase, 1, 0, 1),
        ]
        for group, dt in ((0, 1), (1, -1)):
            base = 2 + 3 * group
            mid = pl.ds(1, slots - 2)
            copies += [
                remote(fps.at[buf, group, mid], fpr.at[buf, group, mid], phase, base, dt, 0),
                remote(fps.at[buf, group, 0], fpr.at[buf, group, 0], phase, base + 1, dt, -1),
                remote(
                    fps.at[buf, group, slots - 1],
                    fpr.at[buf, group, slots - 1],
                    phase,
                    base + 2,
                    dt,
                    1,
                ),
            ]
        for copy in copies:
            copy.start()
        return copies

    def fold(buf, use):
        for group in range(2):
            fpr[buf, group, slots - 2] = fpr[buf, group, slots - 2] + fpr[buf, group, 0]
            fpr[buf, group, 1] = fpr[buf, group, 1] + fpr[buf, group, slots - 1]
        total[buf, pl.ds(RIM, RIM)] = total[buf, pl.ds(RIM, RIM)] + fr[buf, 0]
        total[buf, pl.ds(side, RIM)] = total[buf, pl.ds(side, RIM)] + fr[buf, 1]

        def fold_block(block, slot, first, _):
            kind = kind_of(block, 1, blocks - 2)
            low = fpr[buf, 0, slot]
            high = fpr[buf, 1, slot]
            scale = icov[kind]
            for k in range(RIM):
                row = block * RIM + k
                value = total[buf, row]
                value = value + jnp.where(lane < RIM, unpacked(low, 0, first + k), 0.0)
                value = value + jnp.where(
                    lane >= width - RIM, unpacked(high, RIM, first + k), 0.0
                )
                use(row, value * scale)

        sweep(fold_block, False)

    codes = [orient[my_face, my_tile * tiles + p] for p in range(tiles)]

    def per_lane(values, shape):
        return jnp.where(lax.broadcasted_iota(jnp.int32, shape, 1) < side, values[0], values[1])

    def flips_columns(code):
        return (code == 1) | (code == 2)

    picture_codes = per_lane(codes, (side, width))
    transposes = lax.rem(picture_codes, 2) == 1
    source_lane = lax.broadcasted_iota(jnp.int32, (width, width), 0)
    target_lane = lax.broadcasted_iota(jnp.int32, (width, width), 1)
    tile_start = jnp.where(target_lane < side, 0, side)
    mirrored = 2 * tile_start + side - 1 - target_lane
    wanted = jnp.where(flips_columns(per_lane(codes, (width, width))), mirrored, target_lane)
    swap = jnp.where(source_lane == wanted, 1.0, 0.0).astype(jnp.bfloat16)
    swap = jnp.concatenate([swap, swap, swap], axis=0)

    def flipped(value):
        first = value.astype(jnp.bfloat16)
        rest = value - first.astype(jnp.float32)
        second = rest.astype(jnp.bfloat16)
        third = (rest - second.astype(jnp.float32)).astype(jnp.bfloat16)
        parts = jnp.concatenate([first, second, third], axis=1)
        return jnp.dot(parts, swap, preferred_element_type=jnp.float32)

    def transposed(picture):
        other = jnp.transpose(picture)
        other = jnp.concatenate([other[:side], other[side:]], axis=1)
        return jnp.where(transposes, other, picture)

    def source_row(p, row):
        return jnp.where(codes[p] >= 2, side - 1 - row, row)

    turned_rows[...] = jnp.zeros(turned_rows.shape, jnp.float32)

    def into_rows(field, ex):
        for channel in range(fields):
            picture = flipped(transposed(field[channel]))
            turned_rows[pl.ds(channel, side, stride=PAD)] = picture

        def one_row(row, _):
            first = turned_rows[pl.ds(PAD * source_row(0, row), PAD)]
            second = turned_rows[pl.ds(PAD * source_row(1, row), PAD)]
            ex[row + RIM] = jnp.where(lane < side, first, second)
            return 0

        lax.fori_loop(0, side, one_row, 0)

    into_rows(given, exc)
    cond_copies = start_exchange(exc, 0, 0)
    into_rows(noisy, exs)
    state_copies = start_exchange(exs, 1, 1)
    grid_rows, grid_cols = corners.shape
    next_row = lax.rem(my_face + 1, grid_rows)
    cover_rows = []
    for p in range(tiles):
        here = my_tile * tiles + p
        beside = lax.rem(here + 1, grid_cols)
        cuts = [
            corners[my_face, here],
            corners[my_face, beside],
            corners[next_row, here],
            corners[next_row, beside],
        ]
        col = lax.rem(lane + width - (p * side - RIM), width)
        ones = jnp.where(col < extent, 1.0, 0.0)
        left = col < RIM
        right = (col >= side + RIM) & (col < extent)
        cut_low, cut_high = [
            jnp.where(left, cuts[k], jnp.where(right, cuts[k + 1], 0)) for k in (0, 2)
        ]
        msk[p, 0] = jnp.where(cut_low == 1, 0.0, ones)
        msk[p, 1] = ones
        msk[p, 2] = jnp.where(cut_high == 1, 0.0, ones)
        inner = lane - p * side
        left = inner < RIM
        right = inner >= side - RIM
        band = jnp.where(left | right, 1.0, 0.0)
        cut_low, cut_high = [
            jnp.where(left, cuts[k], jnp.where(right, cuts[k + 1], 1)) for k in (0, 2)
        ]
        cover_rows.append(
            (
                2.0 + band + jnp.where(cut_low == 1, 0.0, 1.0),
                1.0 + band,
                2.0 + band + jnp.where(cut_high == 1, 0.0, 1.0),
            )
        )
        tap_col = lax.broadcasted_iota(jnp.int32, (9 * PAD, 9 * fields), 0)
        tap = tap_col // PAD
        channel = tap_col - tap * PAD
        a = jnp.where(tap >= 6, 2, jnp.where(tap >= 3, 1, 0))
        b = tap - 3 * a
        code = codes[p]
        source_a = jnp.where(
            code == 0, a, jnp.where(code == 3, b, jnp.where(code == 2, 2 - a, 2 - b))
        )
        source_b = jnp.where(
            code == 0, b, jnp.where(code == 3, 2 - a, jnp.where(code == 2, 2 - b, a))
        )
        source = (3 * source_a + source_b) * fields + channel
        place = lax.broadcasted_iota(jnp.int32, (9 * PAD, 9 * fields), 1)
        pick = jnp.where((source == place) & (channel < fields), 1.0, 0.0).astype(jnp.bfloat16)
        for weights, inner_weights in ((wm, ws_t), (wc, wc_t)):
            taps = jnp.dot(pick, inner_weights[...], preferred_element_type=jnp.float32)
            weights[p] = (0.5 * jnp.transpose(taps)).astype(jnp.bfloat16)
        taps = jnp.dot(pick, w_out[...], preferred_element_type=jnp.float32)
        wo[p] = jnp.concatenate(
            [guide_weight * taps, (1.0 - guide_weight) * taps], axis=1
        ).astype(jnp.bfloat16)
    for kind in range(3):
        cover = jnp.where(lane < side, cover_rows[0][kind], cover_rows[1][kind])
        icov[kind] = 1.0 / cover
    for number, embedding in enumerate((e1, e2)):
        spread_out = jnp.broadcast_to(0.5 * embedding[...], (width, hidden))
        emb[number] = jnp.transpose(spread_out)
    finish(cond_copies)
    windows(exc, 0, 1.0)
    features()
    finish(state_copies)
    windows(exs, 1, scale_first)
    predictions(0)
    copies = start_fold(2, 0)
    finish(copies)

    def first_use(row, slope):
        sl1[row - RIM] = slope
        exm[row] = exs[row] + step_size * slope

    fold(0, first_use)
    copies = start_exchange(exm, 3, 2)
    finish(copies)
    windows(exm, 2, scale_second)
    predictions(1)
    copies = start_fold(4, 1)
    finish(copies)

    def second_use(row, slope):
        updated[row - RIM] = exs[row] + 0.5 * step_size * (sl1[row - RIM] + slope)

    fold(1, second_use)

    def turn_block(block, _):
        rows = []
        for k in range(RIM):
            row = block * RIM + k
            first = updated[source_row(0, row)]
            second = updated[source_row(1, row)]
            rows.append(jnp.where(lane < side, first, second))
        start = pl.multiple_of(block * RIM * PAD, RIM * PAD)
        turned_rows[pl.ds(start, RIM * PAD)] = flipped(jnp.concatenate(rows, axis=0))
        return 0

    lax.fori_loop(0, side // RIM, turn_block, 0)
    for channel in range(fields):
        out[channel] = transposed(turned_rows[pl.ds(channel, side, stride=PAD)])


def local(
    noisy_state,
    conditioning,
    orient,
    corner_points,
    w_state,
    w_cond,
    w_out,
    embed_first,
    embed_second,
):
    fields, side, width = noisy_state.shape
    tiles = width // side
    extent = side + 2 * RIM
    hidden = w_state.shape[0]
    slots = (extent // RIM + 2) // 2
    f32 = jnp.float32
    vmem = pl.BlockSpec(memory_space=pltpu.VMEM)
    smem = pl.BlockSpec(memory_space=pltpu.SMEM)
    return pl.pallas_call(
        functools.partial(kernel, side),
        out_shape=jax.ShapeDtypeStruct((fields, side, width), f32),
        in_specs=[vmem, vmem, smem, smem] + [vmem] * 5,
        out_specs=vmem,
        scratch_shapes=[
            pltpu.VMEM((tiles, hidden, 9 * PAD), jnp.bfloat16),
            pltpu.VMEM((tiles, hidden, 9 * PAD), jnp.bfloat16),
            pltpu.VMEM((tiles, 9 * PAD, 2 * hidden), jnp.bfloat16),
            pltpu.VMEM((2, hidden, width), f32),
            pltpu.VMEM((tiles, 3, PAD, width), f32),
            pltpu.VMEM((3, PAD, width), f32),
            pltpu.VMEM((side * PAD, width), f32),
            pltpu.VMEM((side, PAD, width), f32),
            pltpu.VMEM((extent, PAD, width), f32),
            pltpu.VMEM((extent, PAD, width), f32),
            pltpu.VMEM((extent, PAD, width), f32),
            pltpu.VMEM((tiles, 3, extent + 2, PAD, width), jnp.bfloat16),
            pltpu.VMEM((tiles, extent // RIM, hidden, RIM * width), f32),
            pltpu.VMEM((tiles, extent + 1, PAD, width), f32),
            pltpu.VMEM((2, extent, PAD, width), f32),
            pltpu.VMEM((side, PAD, width), f32),
            pltpu.VMEM((3, 2, slots, PAD, width), f32),
            pltpu.VMEM((3, 2, slots, PAD, width), f32),
            pltpu.VMEM((2, 2, RIM, PAD, width), f32),
            pltpu.VMEM((2, 2, slots, PAD, width), f32),
            pltpu.VMEM((2, 2, slots, PAD, width), f32),
            pltpu.SemaphoreType.DMA((5, 8)),
            pltpu.SemaphoreType.DMA((5, 8)),
        ],
        compiler_params=pltpu.CompilerParams(
            collective_id=0, has_side_effects=True, vmem_limit_bytes=50 * 1024 * 1024
        ),
    )(
        noisy_state,
        conditioning,
        orient,
        corner_points,
        w_state.T,
        w_cond.T,
        w_out,
        embed_first[None],
        embed_second[None],
    )


def solution(mesh):
    return jax.shard_map(
        local,
        mesh=mesh,
        in_specs=(
            P("groups", "face", "tile"),
            P("groups", "face", "tile"),
            P(),
            P(),
            P(),
            P(),
            P(),
            P(),
            P(),
        ),
        out_specs=P("groups", "face", "tile"),
        check_vma=False,
    )
```

```python
import functools
import math

import jax
import jax.numpy as jnp
from jax import lax
from jax.experimental import pallas as pl
from jax.experimental.pallas import tpu as pltpu
from jax.sharding import PartitionSpec as P

RIM = 8
PAD = 16
MESH = pl.DeviceIdType.MESH

guide_weight = 2.0
sigma_first = 1.0
sigma_second = 0.6
step_size = sigma_second - sigma_first
scale_first = 1.0 / math.sqrt(1.0 + sigma_first**2)
scale_second = 1.0 / math.sqrt(1.0 + sigma_second**2)


def kernel(
    side,
    noisy_in, given_in, orient, corners, ws_in, wc_in, w_out_in, e1, e2,
    out,
    noisy, given, ws_t, wc_t, w_out, fetched,
    wm, wc, wo, emb, msk, icov, turned_rows, updated,
    exs, exc, exm, win, feat, outs, total, sl1,
    ps, pr, fr, fps, fpr,
    send, recv,
):
    fetches = [
        pltpu.make_async_copy(source, target, fetched.at[number])
        for number, (source, target) in enumerate(
            (
                (given_in, given),
                (noisy_in, noisy),
                (ws_in, ws_t),
                (wc_in, wc_t),
                (w_out_in, w_out),
            )
        )
    ]
    for fetch in fetches:
        fetch.start()
    fields, _, width = noisy.shape
    hidden = w_out.shape[1]
    extent = side + 2 * RIM
    blocks = extent // RIM
    tiles = width // side
    n_tile = lax.axis_size("tile")
    n_face = lax.axis_size("face")
    my_tile = lax.axis_index("tile")
    my_face = lax.axis_index("face")

    def device(d_tile, d_face):
        return {
            "tile": lax.rem(my_tile + d_tile + n_tile, n_tile),
            "face": lax.rem(my_face + d_face + n_face, n_face),
        }

    around = [(dt, df) for dt in (-1, 0, 1) for df in (-1, 0, 1) if (dt, df) != (0, 0)]
    barrier = pltpu.get_barrier_semaphore()
    for dt, df in around:
        pl.semaphore_signal(barrier, inc=1, device_id=device(dt, df), device_id_type=MESH)
    pl.semaphore_wait(barrier, len(around))

    lane = lax.broadcasted_iota(jnp.int32, (PAD, width), 1)
    slots = (blocks + 2) // 2

    def remote(src, dst, phase, number, dt, df):
        return pltpu.make_async_remote_copy(
            src_ref=src,
            dst_ref=dst,
            send_sem=send.at[phase, number],
            recv_sem=recv.at[phase, number],
            device_id=device(dt, df),
            device_id_type=MESH,
        )

    def packed(load, shift, first):
        value = jnp.zeros((PAD, width), jnp.float32)
        for k in range(RIM):
            place = k + first
            moved = pltpu.roll(load(k), (shift + RIM * place) % width, 1)
            value = jnp.where(lane // RIM == place, moved, value)
        return value

    def unpacked(slot, shift, place):
        return pltpu.roll(slot, (-shift - RIM * place) % width, 1)

    def kind_of(block, low, high):
        return jnp.where(block == low, 0, jnp.where(block == high, 2, 1))

    def sweep(visit, ends):
        if ends:
            visit(0, 0, RIM, 0)

        def pair(slot, _):
            visit(2 * slot - 1, slot, 0, 1)
            visit(2 * slot, slot, RIM, 1)
            return 0

        lax.fori_loop(1, slots - 1, pair, 0)
        if ends:
            visit(blocks - 1, slots - 1, 0, 2)

    def start_exchange(ex, phase, buf):
        def pack_block(block, slot, first, _):
            for group in range(2):
                part = packed(lambda k: ex[block * RIM + k], RIM * group, first)
                ps[buf, group, slot] = ps[buf, group, slot] + part

        ps[buf] = jnp.zeros(ps.shape[1:], jnp.float32)
        sweep(pack_block, False)
        copies = [
            remote(ex.at[pl.ds(RIM, RIM)], ex.at[pl.ds(side + RIM, RIM)], phase, 0, 0, -1),
            remote(ex.at[pl.ds(side, RIM)], ex.at[pl.ds(0, RIM)], phase, 1, 0, 1),
        ]
        for group, dt in ((0, -1), (1, 1)):
            base = 2 + 3 * group
            mid = pl.ds(1, slots - 2)
            copies += [
                remote(ps.at[buf, group, mid], pr.at[buf, group, mid], phase, base, dt, 0),
                remote(
                    ps.at[buf, group, 1], pr.at[buf, group, slots - 1], phase, base + 1, dt, -1
                ),
                remote(
                    ps.at[buf, group, slots - 2], pr.at[buf, group, 0], phase, base + 2, dt, 1
                ),
            ]
        for copy in copies:
            copy.start()
        return copies

    def finish(copies):
        for copy in copies:
            copy.wait()

    def windows(ex, buf, scale):
        for p in range(tiles):
            for b in range(3):
                win[p, b, 0] = jnp.zeros((PAD, width), jnp.bfloat16)
                win[p, b, extent + 1] = jnp.zeros((PAD, width), jnp.bfloat16)

        def window_block(block, slot, first, kind):
            after = pr[buf, 0, slot]
            before = pr[buf, 1, slot]
            for k in range(RIM):
                row = block * RIM + k
                body = ex[row]
                left = jnp.where(lane >= width - RIM, unpacked(before, RIM, first + k), body)
                right = jnp.where(lane < RIM, unpacked(after, 0, first + k), body)
                for p, picture in ((0, left), (1, right)):
                    value = jnp.where(msk[p, kind] > 0, scale * picture, 0.0)
                    win[p, 0, row + 1] = pltpu.roll(value, 1, 1).astype(jnp.bfloat16)
                    win[p, 1, row + 1] = value.astype(jnp.bfloat16)
                    win[p, 2, row + 1] = pltpu.roll(value, width - 1, 1).astype(jnp.bfloat16)

        sweep(window_block, True)

    def patch(p, first_row):
        taps = []
        for a in range(3):
            for b in range(3):
                rows = win[p, b, pl.ds(first_row + a, RIM)]
                taps.append(jnp.concatenate([rows[r] for r in range(RIM)], axis=1))
        return jnp.concatenate(taps, axis=0)

    def features():
        def feature_block(step, _):
            p = step // blocks
            block = lax.rem(step, blocks)
            feat[p, block] = jnp.dot(
                wc[p], patch(p, block * RIM), preferred_element_type=jnp.float32
            )
            return 0

        lax.fori_loop(0, tiles * blocks, feature_block, 0)

    def predictions(number):
        group = 3 * PAD

        def finish_row(p, place, taps):
            valid = msk[p, 1]
            outs[p, place] = (
                taps[PAD : 2 * PAD]
                + pltpu.roll(taps[:PAD] * valid, 1, 1)
                + pltpu.roll(taps[2 * PAD :] * valid, width - 1, 1)
            )

        def predict_block(block, carry):
            later = []
            for p in range(tiles):
                pending, above = carry[p]
                mixed = jnp.dot(wm[p], patch(p, block * RIM), preferred_element_type=jnp.float32)
                mixed = mixed + jnp.concatenate([emb[number]] * RIM, axis=1)
                cond = mixed + feat[p, block]
                both = jnp.concatenate([cond, mixed], axis=0).astype(jnp.bfloat16)
                both = both + both * jnp.tanh(both)
                z = jnp.dot(wo[p], both, preferred_element_type=jnp.float32)

                def part(a, r):
                    return z[a * group : (a + 1) * group, r * width : (r + 1) * width]

                start = block * RIM
                finish_row(p, start, pending + part(2, 0))
                finish_row(p, start + 1, above + part(1, 0) + part(2, 1))
                for r in range(1, RIM - 1):
                    finish_row(p, start + 1 + r, part(0, r - 1) + part(1, r) + part(2, r + 1))
                later.append((part(0, RIM - 2) + part(1, RIM - 1), part(0, RIM - 1)))
            return tuple(later)

        none = jnp.zeros((group, width), jnp.float32)
        carry = lax.fori_loop(0, blocks, predict_block, ((none, none),) * tiles)
        for p in range(tiles):
            finish_row(p, extent, carry[p][0])

    def start_fold(phase, buf):
        fps[buf] = jnp.zeros(fps.shape[1:], jnp.float32)

        def spread_block(block, slot, first, kind):
            halves = ([], [])
            for k in range(RIM):
                row = block * RIM + k
                first_out = outs[0, row + 1] * msk[0, kind]
                second_out = outs[1, row + 1] * msk[1, kind]
                total[buf, row] = jnp.where(lane < 3 * width // 4, first_out, 0.0) + jnp.where(
                    lane >= width // 4, second_out, 0.0
                )
                halves[0].append(second_out)
                halves[1].append(first_out)
            for group in range(2):
                part = packed(lambda k: halves[group][k], RIM * group, first)
                fps[buf, group, slot] = fps[buf, group, slot] + part

        sweep(spread_block, True)
        copies = [
            remote(total.at[buf, pl.ds(0, RIM)], fr.at[buf, 1], phase, 0, 0, -1),
            remote(total.at[buf, pl.ds(side + RIM, RIM)], fr.at[buf, 0], phase, 1, 0, 1),
        ]
        for group, dt in ((0, 1), (1, -1)):
            base = 2 + 3 * group
            mid = pl.ds(1, slots - 2)
            copies += [
                remote(fps.at[buf, group, mid], fpr.at[buf, group, mid], phase, base, dt, 0),
                remote(fps.at[buf, group, 0], fpr.at[buf, group, 0], phase, base + 1, dt, -1),
                remote(
                    fps.at[buf, group, slots - 1],
                    fpr.at[buf, group, slots - 1],
                    phase,
                    base + 2,
                    dt,
                    1,
                ),
            ]
        for copy in copies:
            copy.start()
        return copies

    def fold(buf, use):
        for group in range(2):
            fpr[buf, group, slots - 2] = fpr[buf, group, slots - 2] + fpr[buf, group, 0]
            fpr[buf, group, 1] = fpr[buf, group, 1] + fpr[buf, group, slots - 1]
        total[buf, pl.ds(RIM, RIM)] = total[buf, pl.ds(RIM, RIM)] + fr[buf, 0]
        total[buf, pl.ds(side, RIM)] = total[buf, pl.ds(side, RIM)] + fr[buf, 1]

        def fold_block(block, slot, first, _):
            kind = kind_of(block, 1, blocks - 2)
            low = fpr[buf, 0, slot]
            high = fpr[buf, 1, slot]
            scale = icov[kind]
            for k in range(RIM):
                row = block * RIM + k
                value = total[buf, row]
                value = value + jnp.where(lane < RIM, unpacked(low, 0, first + k), 0.0)
                value = value + jnp.where(
                    lane >= width - RIM, unpacked(high, RIM, first + k), 0.0
                )
                use(row, value * scale)

        sweep(fold_block, False)

    codes = [orient[my_face, my_tile * tiles + p] for p in range(tiles)]

    def per_lane(values, shape):
        return jnp.where(lax.broadcasted_iota(jnp.int32, shape, 1) < side, values[0], values[1])

    def flips_columns(code):
        return (code == 1) | (code == 2)

    picture_codes = per_lane(codes, (side, width))
    transposes = lax.rem(picture_codes, 2) == 1
    source_lane = lax.broadcasted_iota(jnp.int32, (width, width), 0)
    target_lane = lax.broadcasted_iota(jnp.int32, (width, width), 1)
    tile_start = jnp.where(target_lane < side, 0, side)
    mirrored = 2 * tile_start + side - 1 - target_lane
    wanted = jnp.where(flips_columns(per_lane(codes, (width, width))), mirrored, target_lane)
    swap = jnp.where(source_lane == wanted, 1.0, 0.0).astype(jnp.bfloat16)
    swap = jnp.concatenate([swap, swap, swap], axis=0)

    def flipped(value):
        first = value.astype(jnp.bfloat16)
        rest = value - first.astype(jnp.float32)
        second = rest.astype(jnp.bfloat16)
        third = (rest - second.astype(jnp.float32)).astype(jnp.bfloat16)
        parts = jnp.concatenate([first, second, third], axis=1)
        return jnp.dot(parts, swap, preferred_element_type=jnp.float32)

    def transposed(picture):
        other = jnp.transpose(picture)
        other = jnp.concatenate([other[:side], other[side:]], axis=1)
        return jnp.where(transposes, other, picture)

    def source_row(p, row):
        return jnp.where(codes[p] >= 2, side - 1 - row, row)

    turned_rows[...] = jnp.zeros(turned_rows.shape, jnp.float32)

    def into_rows(field, ex):
        pictures = [transposed(field[channel]) for channel in range(fields)]
        pictures = flipped(jnp.concatenate(pictures, axis=0))
        for channel in range(fields):
            picture = pictures[channel * side : (channel + 1) * side]
            turned_rows[pl.ds(channel, side, stride=PAD)] = picture

        def some_rows(block, _):
            for k in range(RIM):
                row = block * RIM + k
                first = turned_rows[pl.ds(PAD * source_row(0, row), PAD)]
                second = turned_rows[pl.ds(PAD * source_row(1, row), PAD)]
                ex[row + RIM] = jnp.where(lane < side, first, second)
            return 0

        lax.fori_loop(0, side // RIM, some_rows, 0)

    fetches[0].wait()
    into_rows(given, exc)
    cond_copies = start_exchange(exc, 0, 0)
    fetches[1].wait()
    into_rows(noisy, exs)
    state_copies = start_exchange(exs, 1, 1)
    for fetch in fetches[2:]:
        fetch.wait()
    grid_rows, grid_cols = corners.shape
    next_row = lax.rem(my_face + 1, grid_rows)
    cover_rows = []
    for p in range(tiles):
        here = my_tile * tiles + p
        beside = lax.rem(here + 1, grid_cols)
        cuts = [
            corners[my_face, here],
            corners[my_face, beside],
            corners[next_row, here],
            corners[next_row, beside],
        ]
        col = lax.rem(lane + width - (p * side - RIM), width)
        ones = jnp.where(col < extent, 1.0, 0.0)
        left = col < RIM
        right = (col >= side + RIM) & (col < extent)
        cut_low, cut_high = [
            jnp.where(left, cuts[k], jnp.where(right, cuts[k + 1], 0)) for k in (0, 2)
        ]
        msk[p, 0] = jnp.where(cut_low == 1, 0.0, ones)
        msk[p, 1] = ones
        msk[p, 2] = jnp.where(cut_high == 1, 0.0, ones)
        inner = lane - p * side
        left = inner < RIM
        right = inner >= side - RIM
        band = jnp.where(left | right, 1.0, 0.0)
        cut_low, cut_high = [
            jnp.where(left, cuts[k], jnp.where(right, cuts[k + 1], 1)) for k in (0, 2)
        ]
        cover_rows.append(
            (
                2.0 + band + jnp.where(cut_low == 1, 0.0, 1.0),
                1.0 + band,
                2.0 + band + jnp.where(cut_high == 1, 0.0, 1.0),
            )
        )
        tap_col = lax.broadcasted_iota(jnp.int32, (9 * PAD, 9 * fields), 0)
        tap = tap_col // PAD
        channel = tap_col - tap * PAD
        a = jnp.where(tap >= 6, 2, jnp.where(tap >= 3, 1, 0))
        b = tap - 3 * a
        code = codes[p]
        source_a = jnp.where(
            code == 0, a, jnp.where(code == 3, b, jnp.where(code == 2, 2 - a, 2 - b))
        )
        source_b = jnp.where(
            code == 0, b, jnp.where(code == 3, 2 - a, jnp.where(code == 2, 2 - b, a))
        )
        source = (3 * source_a + source_b) * fields + channel
        place = lax.broadcasted_iota(jnp.int32, (9 * PAD, 9 * fields), 1)
        pick = jnp.where((source == place) & (channel < fields), 1.0, 0.0).astype(jnp.bfloat16)
        for weights, inner_weights in ((wm, ws_t), (wc, wc_t)):
            taps = jnp.dot(pick, inner_weights[...], preferred_element_type=jnp.float32)
            weights[p] = (0.5 * jnp.transpose(taps)).astype(jnp.bfloat16)
        taps = jnp.dot(pick, w_out[...], preferred_element_type=jnp.float32)
        wo[p] = jnp.concatenate(
            [guide_weight * taps, (1.0 - guide_weight) * taps], axis=1
        ).astype(jnp.bfloat16)
    for kind in range(3):
        cover = jnp.where(lane < side, cover_rows[0][kind], cover_rows[1][kind])
        icov[kind] = 1.0 / cover
    for number, embedding in enumerate((e1, e2)):
        spread_out = jnp.broadcast_to(0.5 * embedding[...], (width, hidden))
        emb[number] = jnp.transpose(spread_out)
    finish(cond_copies)
    windows(exc, 0, 1.0)
    features()
    finish(state_copies)
    windows(exs, 1, scale_first)
    predictions(0)
    copies = start_fold(2, 0)
    finish(copies)

    def first_use(row, slope):
        sl1[row - RIM] = slope
        exm[row] = exs[row] + step_size * slope

    fold(0, first_use)
    copies = start_exchange(exm, 3, 2)
    finish(copies)
    windows(exm, 2, scale_second)
    predictions(1)
    copies = start_fold(4, 1)
    finish(copies)

    def second_use(row, slope):
        updated[row - RIM] = exs[row] + 0.5 * step_size * (sl1[row - RIM] + slope)

    fold(1, second_use)

    def turn_block(block, _):
        rows = []
        for k in range(RIM):
            row = block * RIM + k
            first = updated[source_row(0, row)]
            second = updated[source_row(1, row)]
            rows.append(jnp.where(lane < side, first, second))
        start = pl.multiple_of(block * RIM * PAD, RIM * PAD)
        turned_rows[pl.ds(start, RIM * PAD)] = flipped(jnp.concatenate(rows, axis=0))
        return 0

    lax.fori_loop(0, side // RIM, turn_block, 0)
    for channel in range(fields):
        out[channel] = transposed(turned_rows[pl.ds(channel, side, stride=PAD)])


def local(
    noisy_state,
    conditioning,
    orient,
    corner_points,
    w_state,
    w_cond,
    w_out,
    embed_first,
    embed_second,
):
    fields, side, width = noisy_state.shape
    tiles = width // side
    extent = side + 2 * RIM
    hidden = w_state.shape[0]
    slots = (extent // RIM + 2) // 2
    f32 = jnp.float32
    vmem = pl.BlockSpec(memory_space=pltpu.VMEM)
    smem = pl.BlockSpec(memory_space=pltpu.SMEM)
    hbm = pl.BlockSpec(memory_space=pltpu.HBM)
    return pl.pallas_call(
        functools.partial(kernel, side),
        out_shape=jax.ShapeDtypeStruct((fields, side, width), f32),
        in_specs=[hbm, hbm, smem, smem, hbm, hbm, hbm, vmem, vmem],
        out_specs=vmem,
        scratch_shapes=[
            pltpu.VMEM((fields, side, width), f32),
            pltpu.VMEM((fields, side, width), f32),
            pltpu.VMEM((9 * fields, hidden), jnp.bfloat16),
            pltpu.VMEM((9 * fields, hidden), jnp.bfloat16),
            pltpu.VMEM((9 * fields, hidden), jnp.bfloat16),
            pltpu.SemaphoreType.DMA((5,)),
            pltpu.VMEM((tiles, hidden, 9 * PAD), jnp.bfloat16),
            pltpu.VMEM((tiles, hidden, 9 * PAD), jnp.bfloat16),
            pltpu.VMEM((tiles, 9 * PAD, 2 * hidden), jnp.bfloat16),
            pltpu.VMEM((2, hidden, width), f32),
            pltpu.VMEM((tiles, 3, PAD, width), f32),
            pltpu.VMEM((3, PAD, width), f32),
            pltpu.VMEM((side * PAD, width), f32),
            pltpu.VMEM((side, PAD, width), f32),
            pltpu.VMEM((extent, PAD, width), f32),
            pltpu.VMEM((extent, PAD, width), f32),
            pltpu.VMEM((extent, PAD, width), f32),
            pltpu.VMEM((tiles, 3, extent + 2, PAD, width), jnp.bfloat16),
            pltpu.VMEM((tiles, extent // RIM, hidden, RIM * width), f32),
            pltpu.VMEM((tiles, extent + 1, PAD, width), f32),
            pltpu.VMEM((2, extent, PAD, width), f32),
            pltpu.VMEM((side, PAD, width), f32),
            pltpu.VMEM((3, 2, slots, PAD, width), f32),
            pltpu.VMEM((3, 2, slots, PAD, width), f32),
            pltpu.VMEM((2, 2, RIM, PAD, width), f32),
            pltpu.VMEM((2, 2, slots, PAD, width), f32),
            pltpu.VMEM((2, 2, slots, PAD, width), f32),
            pltpu.SemaphoreType.DMA((5, 8)),
            pltpu.SemaphoreType.DMA((5, 8)),
        ],
        compiler_params=pltpu.CompilerParams(
            collective_id=0, has_side_effects=True, vmem_limit_bytes=64 * 1024 * 1024
        ),
    )(
        noisy_state,
        conditioning,
        orient,
        corner_points,
        w_state.T,
        w_cond.T,
        w_out,
        embed_first[None],
        embed_second[None],
    )


def solution(mesh):
    return jax.shard_map(
        local,
        mesh=mesh,
        in_specs=(
            P("groups", "face", "tile"),
            P("groups", "face", "tile"),
            P(),
            P(),
            P(),
            P(),
            P(),
            P(),
            P(),
        ),
        out_specs=P("groups", "face", "tile"),
        check_vma=False,
    )
```

```python
import functools
import math

import jax
import jax.numpy as jnp
from jax import lax
from jax.experimental import pallas as pl
from jax.experimental.pallas import tpu as pltpu
from jax.sharding import PartitionSpec as P

RIM = 8
PAD = 16
CHUNK = 2
MESH = pl.DeviceIdType.MESH

guide_weight = 2.0
sigma_first = 1.0
sigma_second = 0.6
step_size = sigma_second - sigma_first
scale_first = 1.0 / math.sqrt(1.0 + sigma_first**2)
scale_second = 1.0 / math.sqrt(1.0 + sigma_second**2)


def kernel(
    side,
    noisy_in, given_in, orient, corners, ws_in, wc_in, w_out_in, e1, e2,
    out,
    noisy, given, ws_t, wc_t, w_out, fetched,
    wm, wc, wo, emb, msk, icov, turned_rows, updated,
    exs, exc, exm, win, feat, outs, total, sl1,
    ps, pr, fr, fps, fpr,
    send, recv,
):
    fetches = [
        pltpu.make_async_copy(source, target, fetched.at[number])
        for number, (source, target) in enumerate(
            (
                (given_in, given),
                (noisy_in, noisy),
                (ws_in, ws_t),
                (wc_in, wc_t),
                (w_out_in, w_out),
            )
        )
    ]
    for fetch in fetches:
        fetch.start()
    fields, _, width = noisy.shape
    hidden = w_out.shape[1]
    extent = side + 2 * RIM
    blocks = extent // RIM
    tiles = width // side
    n_tile = lax.axis_size("tile")
    n_face = lax.axis_size("face")
    my_tile = lax.axis_index("tile")
    my_face = lax.axis_index("face")

    def device(d_tile, d_face):
        return {
            "tile": lax.rem(my_tile + d_tile + n_tile, n_tile),
            "face": lax.rem(my_face + d_face + n_face, n_face),
        }

    around = [(dt, df) for dt in (-1, 0, 1) for df in (-1, 0, 1) if (dt, df) != (0, 0)]
    barrier = pltpu.get_barrier_semaphore()
    for dt, df in around:
        pl.semaphore_signal(barrier, inc=1, device_id=device(dt, df), device_id_type=MESH)
    pl.semaphore_wait(barrier, len(around))

    lane = lax.broadcasted_iota(jnp.int32, (PAD, width), 1)
    slots = (blocks + 2) // 2

    def remote(src, dst, phase, number, dt, df):
        return pltpu.make_async_remote_copy(
            src_ref=src,
            dst_ref=dst,
            send_sem=send.at[phase, number],
            recv_sem=recv.at[phase, number],
            device_id=device(dt, df),
            device_id_type=MESH,
        )

    def packed(load, shift, first):
        value = jnp.zeros((PAD, width), jnp.float32)
        for k in range(RIM):
            place = k + first
            moved = pltpu.roll(load(k), (shift + RIM * place) % width, 1)
            value = jnp.where(lane // RIM == place, moved, value)
        return value

    def unpacked(slot, shift, place):
        return pltpu.roll(slot, (-shift - RIM * place) % width, 1)

    def kind_of(block, low, high):
        return jnp.where(block == low, 0, jnp.where(block == high, 2, 1))

    def sweep(visit, ends):
        if ends:
            visit(0, 0, RIM, 0)

        def pair(slot, _):
            visit(2 * slot - 1, slot, 0, 1)
            visit(2 * slot, slot, RIM, 1)
            return 0

        lax.fori_loop(1, slots - 1, pair, 0)
        if ends:
            visit(blocks - 1, slots - 1, 0, 2)

    def start_exchange(ex, phase, buf):
        def pack_block(block, slot, first, _):
            for group in range(2):
                part = packed(lambda k: ex[block * RIM + k], RIM * group, first)
                ps[buf, group, slot] = ps[buf, group, slot] + part

        ps[buf] = jnp.zeros(ps.shape[1:], jnp.float32)
        sweep(pack_block, False)
        copies = [
            remote(ex.at[pl.ds(RIM, RIM)], ex.at[pl.ds(side + RIM, RIM)], phase, 0, 0, -1),
            remote(ex.at[pl.ds(side, RIM)], ex.at[pl.ds(0, RIM)], phase, 1, 0, 1),
        ]
        for group, dt in ((0, -1), (1, 1)):
            base = 2 + 3 * group
            mid = pl.ds(1, slots - 2)
            copies += [
                remote(ps.at[buf, group, mid], pr.at[buf, group, mid], phase, base, dt, 0),
                remote(
                    ps.at[buf, group, 1], pr.at[buf, group, slots - 1], phase, base + 1, dt, -1
                ),
                remote(
                    ps.at[buf, group, slots - 2], pr.at[buf, group, 0], phase, base + 2, dt, 1
                ),
            ]
        for copy in copies:
            copy.start()
        return copies

    def finish(copies):
        for copy in copies:
            copy.wait()

    def windows(ex, buf, scale):
        for p in range(tiles):
            for b in range(3):
                win[p, b, 0] = jnp.zeros((PAD, width), jnp.bfloat16)
                win[p, b, extent + 1] = jnp.zeros((PAD, width), jnp.bfloat16)

        def window_block(block, slot, first, kind):
            after = pr[buf, 0, slot]
            before = pr[buf, 1, slot]
            for k in range(RIM):
                row = block * RIM + k
                body = ex[row]
                left = jnp.where(lane >= width - RIM, unpacked(before, RIM, first + k), body)
                right = jnp.where(lane < RIM, unpacked(after, 0, first + k), body)
                for p, picture in ((0, left), (1, right)):
                    value = jnp.where(msk[p, kind] > 0, scale * picture, 0.0)
                    win[p, 0, row + 1] = pltpu.roll(value, 1, 1).astype(jnp.bfloat16)
                    win[p, 1, row + 1] = value.astype(jnp.bfloat16)
                    win[p, 2, row + 1] = pltpu.roll(value, width - 1, 1).astype(jnp.bfloat16)

        sweep(window_block, True)

    def patch(p, first_row, count):
        taps = []
        for a in range(3):
            for b in range(3):
                rows = win[p, b, pl.ds(first_row + a, count)]
                taps.append(jnp.concatenate([rows[r] for r in range(count)], axis=1))
        return jnp.concatenate(taps, axis=0)

    def features():
        def feature_block(step, _):
            p = step // blocks
            block = lax.rem(step, blocks)
            feat[p, block] = jnp.dot(
                wc[p], patch(p, block * RIM, RIM), preferred_element_type=jnp.float32
            )
            return 0

        lax.fori_loop(0, tiles * blocks, feature_block, 0)

    def predictions(number):
        group = 3 * PAD

        def finish_row(p, place, taps):
            valid = msk[p, 1]
            outs[p, place] = (
                taps[PAD : 2 * PAD]
                + pltpu.roll(taps[:PAD] * valid, 1, 1)
                + pltpu.roll(taps[2 * PAD :] * valid, width - 1, 1)
            )

        def predict_block(block, carry):
            start = block * RIM
            chunks = [(p, r) for r in range(0, RIM, CHUNK) for p in range(tiles)]
            products = {}

            def mix(p, r):
                value = jnp.dot(
                    wm[p], patch(p, start + r, CHUNK), preferred_element_type=jnp.float32
                )
                return value + jnp.concatenate([emb[number]] * CHUNK, axis=1)

            def hide(p, r, mixed):
                cond = mixed + feat[p, block, :, pl.ds(r * width, CHUNK * width)]
                plain_hidden = (mixed + mixed * jnp.tanh(mixed)).astype(jnp.bfloat16)
                cond_hidden = (cond + cond * jnp.tanh(cond)).astype(jnp.bfloat16)
                return jnp.concatenate([cond_hidden, plain_hidden], axis=0)

            def project(p, r, both):
                z = jnp.dot(wo[p], both, preferred_element_type=jnp.float32)
                for k in range(CHUNK):
                    products[p, r + k] = z[:, k * width : (k + 1) * width]

            def part(p, a, r):
                return products[p, r][a * group : (a + 1) * group]

            def finish_rows(p, r):
                pending, above = carry[p]
                for row in range(r, r + CHUNK):
                    if row == 0:
                        taps = pending + part(p, 2, 0)
                    elif row == 1:
                        taps = above + part(p, 1, 0) + part(p, 2, 1)
                    else:
                        taps = part(p, 0, row - 2) + part(p, 1, row - 1) + part(p, 2, row)
                    finish_row(p, start + row, taps)

            mixes, hiddens = {}, {}
            for step in range(len(chunks) + 3):
                if step < len(chunks):
                    mixes[step] = mix(*chunks[step])
                if 0 <= step - 2 < len(chunks):
                    project(*chunks[step - 2], hiddens.pop(step - 2))
                if 0 <= step - 1 < len(chunks):
                    hiddens[step - 1] = hide(*chunks[step - 1], mixes.pop(step - 1))
                if 0 <= step - 3 < len(chunks):
                    finish_rows(*chunks[step - 3])
            return tuple(
                (part(p, 0, RIM - 2) + part(p, 1, RIM - 1), part(p, 0, RIM - 1))
                for p in range(tiles)
            )

        none = jnp.zeros((group, width), jnp.float32)
        carry = lax.fori_loop(0, blocks, predict_block, ((none, none),) * tiles)
        for p in range(tiles):
            finish_row(p, extent, carry[p][0])

    def start_fold(phase, buf):
        fps[buf] = jnp.zeros(fps.shape[1:], jnp.float32)

        def spread_block(block, slot, first, kind):
            halves = ([], [])
            for k in range(RIM):
                row = block * RIM + k
                first_out = outs[0, row + 1] * msk[0, kind]
                second_out = outs[1, row + 1] * msk[1, kind]
                total[buf, row] = jnp.where(lane < 3 * width // 4, first_out, 0.0) + jnp.where(
                    lane >= width // 4, second_out, 0.0
                )
                halves[0].append(second_out)
                halves[1].append(first_out)
            for group in range(2):
                part = packed(lambda k: halves[group][k], RIM * group, first)
                fps[buf, group, slot] = fps[buf, group, slot] + part

        sweep(spread_block, True)
        copies = [
            remote(total.at[buf, pl.ds(0, RIM)], fr.at[buf, 1], phase, 0, 0, -1),
            remote(total.at[buf, pl.ds(side + RIM, RIM)], fr.at[buf, 0], phase, 1, 0, 1),
        ]
        for group, dt in ((0, 1), (1, -1)):
            base = 2 + 3 * group
            mid = pl.ds(1, slots - 2)
            copies += [
                remote(fps.at[buf, group, mid], fpr.at[buf, group, mid], phase, base, dt, 0),
                remote(fps.at[buf, group, 0], fpr.at[buf, group, 0], phase, base + 1, dt, -1),
                remote(
                    fps.at[buf, group, slots - 1],
                    fpr.at[buf, group, slots - 1],
                    phase,
                    base + 2,
                    dt,
                    1,
                ),
            ]
        for copy in copies:
            copy.start()
        return copies

    def fold(buf, use):
        for group in range(2):
            fpr[buf, group, slots - 2] = fpr[buf, group, slots - 2] + fpr[buf, group, 0]
            fpr[buf, group, 1] = fpr[buf, group, 1] + fpr[buf, group, slots - 1]
        total[buf, pl.ds(RIM, RIM)] = total[buf, pl.ds(RIM, RIM)] + fr[buf, 0]
        total[buf, pl.ds(side, RIM)] = total[buf, pl.ds(side, RIM)] + fr[buf, 1]

        def fold_block(block, slot, first, _):
            kind = kind_of(block, 1, blocks - 2)
            low = fpr[buf, 0, slot]
            high = fpr[buf, 1, slot]
            scale = icov[kind]
            for k in range(RIM):
                row = block * RIM + k
                value = total[buf, row]
                value = value + jnp.where(lane < RIM, unpacked(low, 0, first + k), 0.0)
                value = value + jnp.where(
                    lane >= width - RIM, unpacked(high, RIM, first + k), 0.0
                )
                use(row, value * scale)

        sweep(fold_block, False)

    codes = [orient[my_face, my_tile * tiles + p] for p in range(tiles)]

    def per_lane(values, shape):
        return jnp.where(lax.broadcasted_iota(jnp.int32, shape, 1) < side, values[0], values[1])

    def flips_columns(code):
        return (code == 1) | (code == 2)

    picture_codes = per_lane(codes, (side, width))
    transposes = lax.rem(picture_codes, 2) == 1
    source_lane = lax.broadcasted_iota(jnp.int32, (width, width), 0)
    target_lane = lax.broadcasted_iota(jnp.int32, (width, width), 1)
    tile_start = jnp.where(target_lane < side, 0, side)
    mirrored = 2 * tile_start + side - 1 - target_lane
    wanted = jnp.where(flips_columns(per_lane(codes, (width, width))), mirrored, target_lane)
    swap = jnp.where(source_lane == wanted, 1.0, 0.0).astype(jnp.bfloat16)
    swap = jnp.concatenate([swap, swap, swap], axis=0)

    def flipped(value):
        first = value.astype(jnp.bfloat16)
        rest = value - first.astype(jnp.float32)
        second = rest.astype(jnp.bfloat16)
        third = (rest - second.astype(jnp.float32)).astype(jnp.bfloat16)
        parts = jnp.concatenate([first, second, third], axis=1)
        return jnp.dot(parts, swap, preferred_element_type=jnp.float32)

    def transposed(picture):
        other = jnp.transpose(picture)
        other = jnp.concatenate([other[:side], other[side:]], axis=1)
        return jnp.where(transposes, other, picture)

    def source_row(p, row):
        return jnp.where(codes[p] >= 2, side - 1 - row, row)

    turned_rows[...] = jnp.zeros(turned_rows.shape, jnp.float32)

    def into_rows(field, ex):
        pictures = [transposed(field[channel]) for channel in range(fields)]
        pictures = flipped(jnp.concatenate(pictures, axis=0))
        for channel in range(fields):
            picture = pictures[channel * side : (channel + 1) * side]
            turned_rows[pl.ds(channel, side, stride=PAD)] = picture

        def some_rows(block, _):
            for k in range(RIM):
                row = block * RIM + k
                first = turned_rows[pl.ds(PAD * source_row(0, row), PAD)]
                second = turned_rows[pl.ds(PAD * source_row(1, row), PAD)]
                ex[row + RIM] = jnp.where(lane < side, first, second)
            return 0

        lax.fori_loop(0, side // RIM, some_rows, 0)

    fetches[0].wait()
    into_rows(given, exc)
    cond_copies = start_exchange(exc, 0, 0)
    fetches[1].wait()
    into_rows(noisy, exs)
    state_copies = start_exchange(exs, 1, 1)
    for fetch in fetches[2:]:
        fetch.wait()
    grid_rows, grid_cols = corners.shape
    next_row = lax.rem(my_face + 1, grid_rows)
    cover_rows = []
    for p in range(tiles):
        here = my_tile * tiles + p
        beside = lax.rem(here + 1, grid_cols)
        cuts = [
            corners[my_face, here],
            corners[my_face, beside],
            corners[next_row, here],
            corners[next_row, beside],
        ]
        col = lax.rem(lane + width - (p * side - RIM), width)
        ones = jnp.where(col < extent, 1.0, 0.0)
        left = col < RIM
        right = (col >= side + RIM) & (col < extent)
        cut_low, cut_high = [
            jnp.where(left, cuts[k], jnp.where(right, cuts[k + 1], 0)) for k in (0, 2)
        ]
        msk[p, 0] = jnp.where(cut_low == 1, 0.0, ones)
        msk[p, 1] = ones
        msk[p, 2] = jnp.where(cut_high == 1, 0.0, ones)
        inner = lane - p * side
        left = inner < RIM
        right = inner >= side - RIM
        band = jnp.where(left | right, 1.0, 0.0)
        cut_low, cut_high = [
            jnp.where(left, cuts[k], jnp.where(right, cuts[k + 1], 1)) for k in (0, 2)
        ]
        cover_rows.append(
            (
                2.0 + band + jnp.where(cut_low == 1, 0.0, 1.0),
                1.0 + band,
                2.0 + band + jnp.where(cut_high == 1, 0.0, 1.0),
            )
        )
        tap_col = lax.broadcasted_iota(jnp.int32, (9 * PAD, 9 * fields), 0)
        tap = tap_col // PAD
        channel = tap_col - tap * PAD
        a = jnp.where(tap >= 6, 2, jnp.where(tap >= 3, 1, 0))
        b = tap - 3 * a
        code = codes[p]
        source_a = jnp.where(
            code == 0, a, jnp.where(code == 3, b, jnp.where(code == 2, 2 - a, 2 - b))
        )
        source_b = jnp.where(
            code == 0, b, jnp.where(code == 3, 2 - a, jnp.where(code == 2, 2 - b, a))
        )
        source = (3 * source_a + source_b) * fields + channel
        place = lax.broadcasted_iota(jnp.int32, (9 * PAD, 9 * fields), 1)
        pick = jnp.where((source == place) & (channel < fields), 1.0, 0.0).astype(jnp.bfloat16)
        for weights, inner_weights in ((wm, ws_t), (wc, wc_t)):
            taps = jnp.dot(pick, inner_weights[...], preferred_element_type=jnp.float32)
            weights[p] = (0.5 * jnp.transpose(taps)).astype(jnp.bfloat16)
        taps = jnp.dot(pick, w_out[...], preferred_element_type=jnp.float32)
        wo[p] = jnp.concatenate(
            [guide_weight * taps, (1.0 - guide_weight) * taps], axis=1
        ).astype(jnp.bfloat16)
    for kind in range(3):
        cover = jnp.where(lane < side, cover_rows[0][kind], cover_rows[1][kind])
        icov[kind] = 1.0 / cover
    for number, embedding in enumerate((e1, e2)):
        spread_out = jnp.broadcast_to(0.5 * embedding[...], (width, hidden))
        emb[number] = jnp.transpose(spread_out)
    finish(cond_copies)
    windows(exc, 0, 1.0)
    features()
    finish(state_copies)
    windows(exs, 1, scale_first)
    predictions(0)
    copies = start_fold(2, 0)
    finish(copies)

    def first_use(row, slope):
        sl1[row - RIM] = slope
        exm[row] = exs[row] + step_size * slope

    fold(0, first_use)
    copies = start_exchange(exm, 3, 2)
    finish(copies)
    windows(exm, 2, scale_second)
    predictions(1)
    copies = start_fold(4, 1)
    finish(copies)

    def second_use(row, slope):
        updated[row - RIM] = exs[row] + 0.5 * step_size * (sl1[row - RIM] + slope)

    fold(1, second_use)

    def turn_block(block, _):
        rows = []
        for k in range(RIM):
            row = block * RIM + k
            first = updated[source_row(0, row)]
            second = updated[source_row(1, row)]
            rows.append(jnp.where(lane < side, first, second))
        start = pl.multiple_of(block * RIM * PAD, RIM * PAD)
        turned_rows[pl.ds(start, RIM * PAD)] = flipped(jnp.concatenate(rows, axis=0))
        return 0

    lax.fori_loop(0, side // RIM, turn_block, 0)
    for channel in range(fields):
        out[channel] = transposed(turned_rows[pl.ds(channel, side, stride=PAD)])


def local(
    noisy_state,
    conditioning,
    orient,
    corner_points,
    w_state,
    w_cond,
    w_out,
    embed_first,
    embed_second,
):
    fields, side, width = noisy_state.shape
    tiles = width // side
    extent = side + 2 * RIM
    hidden = w_state.shape[0]
    slots = (extent // RIM + 2) // 2
    f32 = jnp.float32
    vmem = pl.BlockSpec(memory_space=pltpu.VMEM)
    smem = pl.BlockSpec(memory_space=pltpu.SMEM)
    hbm = pl.BlockSpec(memory_space=pltpu.HBM)
    return pl.pallas_call(
        functools.partial(kernel, side),
        out_shape=jax.ShapeDtypeStruct((fields, side, width), f32),
        in_specs=[hbm, hbm, smem, smem, hbm, hbm, hbm, vmem, vmem],
        out_specs=vmem,
        scratch_shapes=[
            pltpu.VMEM((fields, side, width), f32),
            pltpu.VMEM((fields, side, width), f32),
            pltpu.VMEM((9 * fields, hidden), jnp.bfloat16),
            pltpu.VMEM((9 * fields, hidden), jnp.bfloat16),
            pltpu.VMEM((9 * fields, hidden), jnp.bfloat16),
            pltpu.SemaphoreType.DMA((5,)),
            pltpu.VMEM((tiles, hidden, 9 * PAD), jnp.bfloat16),
            pltpu.VMEM((tiles, hidden, 9 * PAD), jnp.bfloat16),
            pltpu.VMEM((tiles, 9 * PAD, 2 * hidden), jnp.bfloat16),
            pltpu.VMEM((2, hidden, width), f32),
            pltpu.VMEM((tiles, 3, PAD, width), f32),
            pltpu.VMEM((3, PAD, width), f32),
            pltpu.VMEM((side * PAD, width), f32),
            pltpu.VMEM((side, PAD, width), f32),
            pltpu.VMEM((extent, PAD, width), f32),
            pltpu.VMEM((extent, PAD, width), f32),
            pltpu.VMEM((extent, PAD, width), f32),
            pltpu.VMEM((tiles, 3, extent + 2, PAD, width), jnp.bfloat16),
            pltpu.VMEM((tiles, extent // RIM, hidden, RIM * width), f32),
            pltpu.VMEM((tiles, extent + 1, PAD, width), f32),
            pltpu.VMEM((2, extent, PAD, width), f32),
            pltpu.VMEM((side, PAD, width), f32),
            pltpu.VMEM((3, 2, slots, PAD, width), f32),
            pltpu.VMEM((3, 2, slots, PAD, width), f32),
            pltpu.VMEM((2, 2, RIM, PAD, width), f32),
            pltpu.VMEM((2, 2, slots, PAD, width), f32),
            pltpu.VMEM((2, 2, slots, PAD, width), f32),
            pltpu.SemaphoreType.DMA((5, 8)),
            pltpu.SemaphoreType.DMA((5, 8)),
        ],
        compiler_params=pltpu.CompilerParams(
            collective_id=0, has_side_effects=True, vmem_limit_bytes=64 * 1024 * 1024
        ),
    )(
        noisy_state,
        conditioning,
        orient,
        corner_points,
        w_state.T,
        w_cond.T,
        w_out,
        embed_first[None],
        embed_second[None],
    )


def solution(mesh):
    return jax.shard_map(
        local,
        mesh=mesh,
        in_specs=(
            P("groups", "face", "tile"),
            P("groups", "face", "tile"),
            P(),
            P(),
            P(),
            P(),
            P(),
            P(),
            P(),
        ),
        out_specs=P("groups", "face", "tile"),
        check_vma=False,
    )
```

```python
import functools
import math

import jax
import jax.numpy as jnp
from jax import lax
from jax.experimental import pallas as pl
from jax.experimental.pallas import tpu as pltpu
from jax.sharding import PartitionSpec as P

RIM = 8
PAD = 16
CHUNK = 2
MESH = pl.DeviceIdType.MESH

guide_weight = 2.0
sigma_first = 1.0
sigma_second = 0.6
step_size = sigma_second - sigma_first
scale_first = 1.0 / math.sqrt(1.0 + sigma_first**2)
scale_second = 1.0 / math.sqrt(1.0 + sigma_second**2)


def silu(value):
    grown = jnp.exp(jnp.minimum(-value, 80.0))
    return (value * pl.reciprocal(1.0 + grown, approx=True)).astype(jnp.bfloat16)


def kernel(
    side,
    noisy_in, given_in, orient, corners, ws_in, wc_in, w_out_in, e1, e2,
    out,
    noisy, given, ws_t, wc_t, w_out, fetched,
    wm, wc, wo, emb, msk, icov, turned_rows, updated,
    exs, exc, exm, win, feat, outs, total, sl1,
    ps, pr, fr, fps, fpr,
    send, recv,
):
    fetches = [
        pltpu.make_async_copy(source, target, fetched.at[number])
        for number, (source, target) in enumerate(
            (
                (given_in, given),
                (noisy_in, noisy),
                (ws_in, ws_t),
                (wc_in, wc_t),
                (w_out_in, w_out),
            )
        )
    ]
    for fetch in fetches:
        fetch.start()
    fields, _, width = noisy.shape
    hidden = w_out.shape[1]
    extent = side + 2 * RIM
    blocks = extent // RIM
    tiles = width // side
    n_tile = lax.axis_size("tile")
    n_face = lax.axis_size("face")
    my_tile = lax.axis_index("tile")
    my_face = lax.axis_index("face")

    def device(d_tile, d_face):
        return {
            "tile": lax.rem(my_tile + d_tile + n_tile, n_tile),
            "face": lax.rem(my_face + d_face + n_face, n_face),
        }

    around = [(dt, df) for dt in (-1, 0, 1) for df in (-1, 0, 1) if (dt, df) != (0, 0)]
    barrier = pltpu.get_barrier_semaphore()
    for dt, df in around:
        pl.semaphore_signal(barrier, inc=1, device_id=device(dt, df), device_id_type=MESH)
    lane = lax.broadcasted_iota(jnp.int32, (PAD, width), 1)
    slots = (blocks + 2) // 2

    def remote(src, dst, phase, number, dt, df):
        return pltpu.make_async_remote_copy(
            src_ref=src,
            dst_ref=dst,
            send_sem=send.at[phase, number],
            recv_sem=recv.at[phase, number],
            device_id=device(dt, df),
            device_id_type=MESH,
        )

    def packed(load, shift, first):
        value = jnp.zeros((PAD, width), jnp.float32)
        for k in range(RIM):
            place = k + first
            moved = pltpu.roll(load(k), (shift + RIM * place) % width, 1)
            value = jnp.where(lane // RIM == place, moved, value)
        return value

    def unpacked(slot, shift, place):
        return pltpu.roll(slot, (-shift - RIM * place) % width, 1)

    def kind_of(block, low, high):
        return jnp.where(block == low, 0, jnp.where(block == high, 2, 1))

    def sweep(visit, ends):
        if ends:
            visit(0, 0, RIM, 0)

        def pair(slot, _):
            visit(2 * slot - 1, slot, 0, 1)
            visit(2 * slot, slot, RIM, 1)
            return 0

        lax.fori_loop(1, slots - 1, pair, 0)
        if ends:
            visit(blocks - 1, slots - 1, 0, 2)

    def start_exchange(ex, phase, buf):
        def pack_block(block, slot, first, _):
            for group in range(2):
                part = packed(lambda k: ex[block * RIM + k], RIM * group, first)
                ps[buf, group, slot] = ps[buf, group, slot] + part

        ps[buf] = jnp.zeros(ps.shape[1:], jnp.float32)
        sweep(pack_block, False)
        copies = [
            remote(ex.at[pl.ds(RIM, RIM)], ex.at[pl.ds(side + RIM, RIM)], phase, 0, 0, -1),
            remote(ex.at[pl.ds(side, RIM)], ex.at[pl.ds(0, RIM)], phase, 1, 0, 1),
        ]
        for group, dt in ((0, -1), (1, 1)):
            base = 2 + 3 * group
            mid = pl.ds(1, slots - 2)
            copies += [
                remote(ps.at[buf, group, mid], pr.at[buf, group, mid], phase, base, dt, 0),
                remote(
                    ps.at[buf, group, 1], pr.at[buf, group, slots - 1], phase, base + 1, dt, -1
                ),
                remote(
                    ps.at[buf, group, slots - 2], pr.at[buf, group, 0], phase, base + 2, dt, 1
                ),
            ]
        for copy in copies:
            copy.start()
        return copies

    def finish(copies):
        for copy in copies:
            copy.wait()

    def windows(ex, buf, scale):
        for p in range(tiles):
            for b in range(3):
                win[p, b, 0] = jnp.zeros((PAD, width), jnp.bfloat16)
                win[p, b, extent + 1] = jnp.zeros((PAD, width), jnp.bfloat16)

        def window_block(block, slot, first, kind):
            after = pr[buf, 0, slot]
            before = pr[buf, 1, slot]
            for k in range(RIM):
                row = block * RIM + k
                body = ex[row]
                left = jnp.where(lane >= width - RIM, unpacked(before, RIM, first + k), body)
                right = jnp.where(lane < RIM, unpacked(after, 0, first + k), body)
                for p, picture in ((0, left), (1, right)):
                    value = jnp.where(msk[p, kind] > 0, scale * picture, 0.0)
                    win[p, 0, row + 1] = pltpu.roll(value, 1, 1).astype(jnp.bfloat16)
                    win[p, 1, row + 1] = value.astype(jnp.bfloat16)
                    win[p, 2, row + 1] = pltpu.roll(value, width - 1, 1).astype(jnp.bfloat16)

        sweep(window_block, True)

    def patch(p, first_row, count):
        taps = []
        for a in range(3):
            for b in range(3):
                rows = win[p, b, pl.ds(first_row + a, count)]
                taps.append(jnp.concatenate([rows[r] for r in range(count)], axis=1))
        return jnp.concatenate(taps, axis=0)

    def features():
        def feature_block(step, _):
            p = step // blocks
            block = lax.rem(step, blocks)
            feat[p, block] = jnp.dot(
                wc[p], patch(p, block * RIM, RIM), preferred_element_type=jnp.float32
            )
            return 0

        lax.fori_loop(0, tiles * blocks, feature_block, 0)

    def predictions(number):
        group = 3 * PAD

        def finish_row(p, place, taps):
            valid = msk[p, 1]
            outs[p, place] = (
                taps[PAD : 2 * PAD]
                + pltpu.roll(taps[:PAD] * valid, 1, 1)
                + pltpu.roll(taps[2 * PAD :] * valid, width - 1, 1)
            )

        def predict_block(block, carry):
            start = block * RIM
            chunks = [(p, r) for r in range(0, RIM, CHUNK) for p in range(tiles)]
            products = {}

            def mix(p, r):
                value = jnp.dot(
                    wm[p], patch(p, start + r, CHUNK), preferred_element_type=jnp.float32
                )
                return value + jnp.concatenate([emb[number]] * CHUNK, axis=1)

            def hide(p, r, mixed):
                cond = mixed + feat[p, block, :, pl.ds(r * width, CHUNK * width)]
                return jnp.concatenate([silu(cond), silu(mixed)], axis=0)

            def project(p, r, both):
                z = jnp.dot(wo[p], both, preferred_element_type=jnp.float32)
                for k in range(CHUNK):
                    products[p, r + k] = z[:, k * width : (k + 1) * width]

            def part(p, a, r):
                return products[p, r][a * group : (a + 1) * group]

            def finish_rows(p, r):
                pending, above = carry[p]
                for row in range(r, r + CHUNK):
                    if row == 0:
                        taps = pending + part(p, 2, 0)
                    elif row == 1:
                        taps = above + part(p, 1, 0) + part(p, 2, 1)
                    else:
                        taps = part(p, 0, row - 2) + part(p, 1, row - 1) + part(p, 2, row)
                    finish_row(p, start + row, taps)

            mixes, hiddens = {}, {}
            for step in range(len(chunks) + 3):
                if step < len(chunks):
                    mixes[step] = mix(*chunks[step])
                if 0 <= step - 2 < len(chunks):
                    project(*chunks[step - 2], hiddens.pop(step - 2))
                if 0 <= step - 1 < len(chunks):
                    hiddens[step - 1] = hide(*chunks[step - 1], mixes.pop(step - 1))
                if 0 <= step - 3 < len(chunks):
                    finish_rows(*chunks[step - 3])
            return tuple(
                (part(p, 0, RIM - 2) + part(p, 1, RIM - 1), part(p, 0, RIM - 1))
                for p in range(tiles)
            )

        none = jnp.zeros((group, width), jnp.float32)
        carry = lax.fori_loop(0, blocks, predict_block, ((none, none),) * tiles)
        for p in range(tiles):
            finish_row(p, extent, carry[p][0])

    def start_fold(phase, buf):
        fps[buf] = jnp.zeros(fps.shape[1:], jnp.float32)

        def spread_block(block, slot, first, kind):
            halves = ([], [])
            for k in range(RIM):
                row = block * RIM + k
                first_out = outs[0, row + 1] * msk[0, kind]
                second_out = outs[1, row + 1] * msk[1, kind]
                total[buf, row] = jnp.where(lane < 3 * width // 4, first_out, 0.0) + jnp.where(
                    lane >= width // 4, second_out, 0.0
                )
                halves[0].append(second_out)
                halves[1].append(first_out)
            for group in range(2):
                part = packed(lambda k: halves[group][k], RIM * group, first)
                fps[buf, group, slot] = fps[buf, group, slot] + part

        sweep(spread_block, True)
        copies = [
            remote(total.at[buf, pl.ds(0, RIM)], fr.at[buf, 1], phase, 0, 0, -1),
            remote(total.at[buf, pl.ds(side + RIM, RIM)], fr.at[buf, 0], phase, 1, 0, 1),
        ]
        for group, dt in ((0, 1), (1, -1)):
            base = 2 + 3 * group
            mid = pl.ds(1, slots - 2)
            copies += [
                remote(fps.at[buf, group, mid], fpr.at[buf, group, mid], phase, base, dt, 0),
                remote(fps.at[buf, group, 0], fpr.at[buf, group, 0], phase, base + 1, dt, -1),
                remote(
                    fps.at[buf, group, slots - 1],
                    fpr.at[buf, group, slots - 1],
                    phase,
                    base + 2,
                    dt,
                    1,
                ),
            ]
        for copy in copies:
            copy.start()
        return copies

    def fold(buf, use):
        for group in range(2):
            fpr[buf, group, slots - 2] = fpr[buf, group, slots - 2] + fpr[buf, group, 0]
            fpr[buf, group, 1] = fpr[buf, group, 1] + fpr[buf, group, slots - 1]
        total[buf, pl.ds(RIM, RIM)] = total[buf, pl.ds(RIM, RIM)] + fr[buf, 0]
        total[buf, pl.ds(side, RIM)] = total[buf, pl.ds(side, RIM)] + fr[buf, 1]

        def fold_block(block, slot, first, _):
            kind = kind_of(block, 1, blocks - 2)
            low = fpr[buf, 0, slot]
            high = fpr[buf, 1, slot]
            scale = icov[kind]
            for k in range(RIM):
                row = block * RIM + k
                value = total[buf, row]
                value = value + jnp.where(lane < RIM, unpacked(low, 0, first + k), 0.0)
                value = value + jnp.where(
                    lane >= width - RIM, unpacked(high, RIM, first + k), 0.0
                )
                use(row, value * scale)

        sweep(fold_block, False)

    codes = [orient[my_face, my_tile * tiles + p] for p in range(tiles)]

    def per_lane(values, shape):
        return jnp.where(lax.broadcasted_iota(jnp.int32, shape, 1) < side, values[0], values[1])

    def flips_columns(code):
        return (code == 1) | (code == 2)

    picture_codes = per_lane(codes, (side, width))
    transposes = lax.rem(picture_codes, 2) == 1
    source_lane = lax.broadcasted_iota(jnp.int32, (width, width), 0)
    target_lane = lax.broadcasted_iota(jnp.int32, (width, width), 1)
    tile_start = jnp.where(target_lane < side, 0, side)
    mirrored = 2 * tile_start + side - 1 - target_lane
    wanted = jnp.where(flips_columns(per_lane(codes, (width, width))), mirrored, target_lane)
    swap = jnp.where(source_lane == wanted, 1.0, 0.0).astype(jnp.bfloat16)
    swap = jnp.concatenate([swap, swap, swap], axis=0)

    def flipped(value):
        first = value.astype(jnp.bfloat16)
        rest = value - first.astype(jnp.float32)
        second = rest.astype(jnp.bfloat16)
        third = (rest - second.astype(jnp.float32)).astype(jnp.bfloat16)
        parts = jnp.concatenate([first, second, third], axis=1)
        return jnp.dot(parts, swap, preferred_element_type=jnp.float32)

    def transposed(picture):
        other = jnp.transpose(picture)
        other = jnp.concatenate([other[:side], other[side:]], axis=1)
        return jnp.where(transposes, other, picture)

    def source_row(p, row):
        return jnp.where(codes[p] >= 2, side - 1 - row, row)

    turned_rows[...] = jnp.zeros(turned_rows.shape, jnp.float32)

    def into_rows(field, ex):
        pictures = [transposed(field[channel]) for channel in range(fields)]
        pictures = flipped(jnp.concatenate(pictures, axis=0))
        for channel in range(fields):
            picture = pictures[channel * side : (channel + 1) * side]
            turned_rows[pl.ds(channel, side, stride=PAD)] = picture

        def some_rows(block, _):
            for k in range(RIM):
                row = block * RIM + k
                first = turned_rows[pl.ds(PAD * source_row(0, row), PAD)]
                second = turned_rows[pl.ds(PAD * source_row(1, row), PAD)]
                ex[row + RIM] = jnp.where(lane < side, first, second)
            return 0

        lax.fori_loop(0, side // RIM, some_rows, 0)

    fetches[0].wait()
    into_rows(given, exc)
    pl.semaphore_wait(barrier, len(around))
    cond_copies = start_exchange(exc, 0, 0)
    fetches[1].wait()
    into_rows(noisy, exs)
    state_copies = start_exchange(exs, 1, 1)
    for fetch in fetches[2:]:
        fetch.wait()
    grid_rows, grid_cols = corners.shape
    next_row = lax.rem(my_face + 1, grid_rows)
    cover_rows = []
    for p in range(tiles):
        here = my_tile * tiles + p
        beside = lax.rem(here + 1, grid_cols)
        cuts = [
            corners[my_face, here],
            corners[my_face, beside],
            corners[next_row, here],
            corners[next_row, beside],
        ]
        col = lax.rem(lane + width - (p * side - RIM), width)
        ones = jnp.where(col < extent, 1.0, 0.0)
        left = col < RIM
        right = (col >= side + RIM) & (col < extent)
        cut_low, cut_high = [
            jnp.where(left, cuts[k], jnp.where(right, cuts[k + 1], 0)) for k in (0, 2)
        ]
        msk[p, 0] = jnp.where(cut_low == 1, 0.0, ones)
        msk[p, 1] = ones
        msk[p, 2] = jnp.where(cut_high == 1, 0.0, ones)
        inner = lane - p * side
        left = inner < RIM
        right = inner >= side - RIM
        band = jnp.where(left | right, 1.0, 0.0)
        cut_low, cut_high = [
            jnp.where(left, cuts[k], jnp.where(right, cuts[k + 1], 1)) for k in (0, 2)
        ]
        cover_rows.append(
            (
                2.0 + band + jnp.where(cut_low == 1, 0.0, 1.0),
                1.0 + band,
                2.0 + band + jnp.where(cut_high == 1, 0.0, 1.0),
            )
        )
        tap_col = lax.broadcasted_iota(jnp.int32, (9 * PAD, 9 * fields), 0)
        tap = tap_col // PAD
        channel = tap_col - tap * PAD
        a = jnp.where(tap >= 6, 2, jnp.where(tap >= 3, 1, 0))
        b = tap - 3 * a
        code = codes[p]
        source_a = jnp.where(
            code == 0, a, jnp.where(code == 3, b, jnp.where(code == 2, 2 - a, 2 - b))
        )
        source_b = jnp.where(
            code == 0, b, jnp.where(code == 3, 2 - a, jnp.where(code == 2, 2 - b, a))
        )
        source = (3 * source_a + source_b) * fields + channel
        place = lax.broadcasted_iota(jnp.int32, (9 * PAD, 9 * fields), 1)
        pick = jnp.where((source == place) & (channel < fields), 1.0, 0.0).astype(jnp.bfloat16)
        for weights, inner_weights in ((wm, ws_t), (wc, wc_t)):
            taps = jnp.dot(pick, inner_weights[...], preferred_element_type=jnp.float32)
            weights[p] = jnp.transpose(taps).astype(jnp.bfloat16)
        taps = jnp.dot(pick, w_out[...], preferred_element_type=jnp.float32)
        wo[p] = jnp.concatenate(
            [guide_weight * taps, (1.0 - guide_weight) * taps], axis=1
        ).astype(jnp.bfloat16)
    for kind in range(3):
        cover = jnp.where(lane < side, cover_rows[0][kind], cover_rows[1][kind])
        icov[kind] = 1.0 / cover
    for number, embedding in enumerate((e1, e2)):
        spread_out = jnp.broadcast_to(embedding[...], (width, hidden))
        emb[number] = jnp.transpose(spread_out)
    finish(cond_copies)
    windows(exc, 0, 1.0)
    features()
    finish(state_copies)
    windows(exs, 1, scale_first)
    predictions(0)
    copies = start_fold(2, 0)
    finish(copies)

    def first_use(row, slope):
        sl1[row - RIM] = slope
        exm[row] = exs[row] + step_size * slope

    fold(0, first_use)
    copies = start_exchange(exm, 3, 2)
    finish(copies)
    windows(exm, 2, scale_second)
    predictions(1)
    copies = start_fold(4, 1)
    finish(copies)

    def second_use(row, slope):
        updated[row - RIM] = exs[row] + 0.5 * step_size * (sl1[row - RIM] + slope)

    fold(1, second_use)

    def turn_block(block, _):
        rows = []
        for k in range(RIM):
            row = block * RIM + k
            first = updated[source_row(0, row)]
            second = updated[source_row(1, row)]
            rows.append(jnp.where(lane < side, first, second))
        start = pl.multiple_of(block * RIM * PAD, RIM * PAD)
        turned_rows[pl.ds(start, RIM * PAD)] = flipped(jnp.concatenate(rows, axis=0))
        return 0

    lax.fori_loop(0, side // RIM, turn_block, 0)
    for channel in range(fields):
        out[channel] = transposed(turned_rows[pl.ds(channel, side, stride=PAD)])


def local(
    noisy_state,
    conditioning,
    orient,
    corner_points,
    w_state,
    w_cond,
    w_out,
    embed_first,
    embed_second,
):
    fields, side, width = noisy_state.shape
    tiles = width // side
    extent = side + 2 * RIM
    hidden = w_state.shape[0]
    slots = (extent // RIM + 2) // 2
    f32 = jnp.float32
    vmem = pl.BlockSpec(memory_space=pltpu.VMEM)
    smem = pl.BlockSpec(memory_space=pltpu.SMEM)
    hbm = pl.BlockSpec(memory_space=pltpu.HBM)
    return pl.pallas_call(
        functools.partial(kernel, side),
        out_shape=jax.ShapeDtypeStruct((fields, side, width), f32),
        in_specs=[hbm, hbm, smem, smem, hbm, hbm, hbm, vmem, vmem],
        out_specs=vmem,
        scratch_shapes=[
            pltpu.VMEM((fields, side, width), f32),
            pltpu.VMEM((fields, side, width), f32),
            pltpu.VMEM((9 * fields, hidden), jnp.bfloat16),
            pltpu.VMEM((9 * fields, hidden), jnp.bfloat16),
            pltpu.VMEM((9 * fields, hidden), jnp.bfloat16),
            pltpu.SemaphoreType.DMA((5,)),
            pltpu.VMEM((tiles, hidden, 9 * PAD), jnp.bfloat16),
            pltpu.VMEM((tiles, hidden, 9 * PAD), jnp.bfloat16),
            pltpu.VMEM((tiles, 9 * PAD, 2 * hidden), jnp.bfloat16),
            pltpu.VMEM((2, hidden, width), f32),
            pltpu.VMEM((tiles, 3, PAD, width), f32),
            pltpu.VMEM((3, PAD, width), f32),
            pltpu.VMEM((side * PAD, width), f32),
            pltpu.VMEM((side, PAD, width), f32),
            pltpu.VMEM((extent, PAD, width), f32),
            pltpu.VMEM((extent, PAD, width), f32),
            pltpu.VMEM((extent, PAD, width), f32),
            pltpu.VMEM((tiles, 3, extent + 2, PAD, width), jnp.bfloat16),
            pltpu.VMEM((tiles, extent // RIM, hidden, RIM * width), f32),
            pltpu.VMEM((tiles, extent + 1, PAD, width), f32),
            pltpu.VMEM((2, extent, PAD, width), f32),
            pltpu.VMEM((side, PAD, width), f32),
            pltpu.VMEM((3, 2, slots, PAD, width), f32),
            pltpu.VMEM((3, 2, slots, PAD, width), f32),
            pltpu.VMEM((2, 2, RIM, PAD, width), f32),
            pltpu.VMEM((2, 2, slots, PAD, width), f32),
            pltpu.VMEM((2, 2, slots, PAD, width), f32),
            pltpu.SemaphoreType.DMA((5, 8)),
            pltpu.SemaphoreType.DMA((5, 8)),
        ],
        compiler_params=pltpu.CompilerParams(
            collective_id=0, has_side_effects=True, vmem_limit_bytes=64 * 1024 * 1024
        ),
    )(
        noisy_state,
        conditioning,
        orient,
        corner_points,
        w_state.T,
        w_cond.T,
        w_out,
        embed_first[None],
        embed_second[None],
    )


def solution(mesh):
    return jax.shard_map(
        local,
        mesh=mesh,
        in_specs=(
            P("groups", "face", "tile"),
            P("groups", "face", "tile"),
            P(),
            P(),
            P(),
            P(),
            P(),
            P(),
            P(),
        ),
        out_specs=P("groups", "face", "tile"),
        check_vma=False,
    )
```

```python
import functools
import math

import jax
import jax.numpy as jnp
from jax import lax
from jax.experimental import pallas as pl
from jax.experimental.pallas import tpu as pltpu
from jax.sharding import PartitionSpec as P

RIM = 8
PAD = 16
CHUNK = 2
MESH = pl.DeviceIdType.MESH

guide_weight = 2.0
sigma_first = 1.0
sigma_second = 0.6
step_size = sigma_second - sigma_first
scale_first = 1.0 / math.sqrt(1.0 + sigma_first**2)
scale_second = 1.0 / math.sqrt(1.0 + sigma_second**2)


def silu(value):
    return (value + value * jnp.tanh(value)).astype(jnp.bfloat16)


def kernel(
    side,
    noisy_in, given_in, orient, corners, ws_in, wc_in, w_out_in, e1, e2,
    out,
    noisy, given, ws_t, wc_t, w_out, fetched,
    wm, wc, wo, emb, msk, icov, turned_rows, updated,
    exs, exc, exm, win, feat, outs, total, sl1,
    ps, pr, fr, fps, fpr,
    send, recv,
):
    fetches = [
        pltpu.make_async_copy(source, target, fetched.at[number])
        for number, (source, target) in enumerate(
            (
                (given_in, given),
                (noisy_in, noisy),
                (ws_in, ws_t),
                (wc_in, wc_t),
                (w_out_in, w_out),
            )
        )
    ]
    for fetch in fetches:
        fetch.start()
    fields, _, width = noisy.shape
    hidden = w_out.shape[1]
    extent = side + 2 * RIM
    blocks = extent // RIM
    tiles = width // side
    n_tile = lax.axis_size("tile")
    n_face = lax.axis_size("face")
    my_tile = lax.axis_index("tile")
    my_face = lax.axis_index("face")

    def device(d_tile, d_face):
        return {
            "tile": lax.rem(my_tile + d_tile + n_tile, n_tile),
            "face": lax.rem(my_face + d_face + n_face, n_face),
        }

    around = [(dt, df) for dt in (-1, 0, 1) for df in (-1, 0, 1) if (dt, df) != (0, 0)]
    barrier = pltpu.get_barrier_semaphore()
    for dt, df in around:
        pl.semaphore_signal(barrier, inc=1, device_id=device(dt, df), device_id_type=MESH)
    lane = lax.broadcasted_iota(jnp.int32, (PAD, width), 1)
    slots = (blocks + 2) // 2

    def remote(src, dst, phase, number, dt, df):
        return pltpu.make_async_remote_copy(
            src_ref=src,
            dst_ref=dst,
            send_sem=send.at[phase, number],
            recv_sem=recv.at[phase, number],
            device_id=device(dt, df),
            device_id_type=MESH,
        )

    def packed(load, shift, first):
        value = jnp.zeros((PAD, width), jnp.float32)
        for k in range(RIM):
            place = k + first
            moved = pltpu.roll(load(k), (shift + RIM * place) % width, 1)
            inside = (lane >= RIM * place) & (lane < RIM * (place + 1))
            value = jnp.where(inside, moved, value)
        return value

    def unpacked(slot, shift, place):
        return pltpu.roll(slot, (-shift - RIM * place) % width, 1)

    def kind_of(block, low, high):
        return jnp.where(block == low, 0, jnp.where(block == high, 2, 1))

    def sweep(visit, ends):
        if ends:
            visit(0, 0, RIM, 0)

        def pair(slot, _):
            visit(2 * slot - 1, slot, 0, 1)
            visit(2 * slot, slot, RIM, 1)
            return 0

        lax.fori_loop(1, slots - 1, pair, 0)
        if ends:
            visit(blocks - 1, slots - 1, 0, 2)

    def start_exchange(ex, phase, buf):
        def pack_block(block, slot, first, _):
            for group in range(2):
                part = packed(lambda k: ex[block * RIM + k], RIM * group, first)
                ps[buf, group, slot] = ps[buf, group, slot] + part

        ps[buf] = jnp.zeros(ps.shape[1:], jnp.float32)
        sweep(pack_block, False)
        copies = [
            remote(ex.at[pl.ds(RIM, RIM)], ex.at[pl.ds(side + RIM, RIM)], phase, 0, 0, -1),
            remote(ex.at[pl.ds(side, RIM)], ex.at[pl.ds(0, RIM)], phase, 1, 0, 1),
        ]
        for group, dt in ((0, -1), (1, 1)):
            base = 2 + 3 * group
            mid = pl.ds(1, slots - 2)
            copies += [
                remote(ps.at[buf, group, mid], pr.at[buf, group, mid], phase, base, dt, 0),
                remote(
                    ps.at[buf, group, 1], pr.at[buf, group, slots - 1], phase, base + 1, dt, -1
                ),
                remote(
                    ps.at[buf, group, slots - 2], pr.at[buf, group, 0], phase, base + 2, dt, 1
                ),
            ]
        for copy in copies:
            copy.start()
        return copies

    def finish(copies):
        for copy in copies:
            copy.wait()

    def windows(ex, buf, scale):
        for p in range(tiles):
            for b in range(3):
                win[p, b, 0] = jnp.zeros((PAD, width), jnp.bfloat16)
                win[p, b, extent + 1] = jnp.zeros((PAD, width), jnp.bfloat16)

        def window_block(block, slot, first, kind):
            after = pr[buf, 0, slot]
            before = pr[buf, 1, slot]
            for k in range(RIM):
                row = block * RIM + k
                body = ex[row]
                left = jnp.where(lane >= width - RIM, unpacked(before, RIM, first + k), body)
                right = jnp.where(lane < RIM, unpacked(after, 0, first + k), body)
                for p, picture in ((0, left), (1, right)):
                    value = jnp.where(msk[p, kind] > 0, scale * picture, 0.0)
                    win[p, 0, row + 1] = pltpu.roll(value, 1, 1).astype(jnp.bfloat16)
                    win[p, 1, row + 1] = value.astype(jnp.bfloat16)
                    win[p, 2, row + 1] = pltpu.roll(value, width - 1, 1).astype(jnp.bfloat16)

        sweep(window_block, True)

    def patch(p, first_row, count):
        taps = []
        for a in range(3):
            for b in range(3):
                rows = win[p, b, pl.ds(first_row + a, count)]
                taps.append(jnp.concatenate([rows[r] for r in range(count)], axis=1))
        return jnp.concatenate(taps, axis=0)

    def features():
        def feature_block(block, _):
            for p in range(tiles):
                feat[p, block] = jnp.dot(
                    wc[p], patch(p, block * RIM, RIM), preferred_element_type=jnp.float32
                )
            return 0

        lax.fori_loop(0, blocks, feature_block, 0)

    def predictions(number):
        group = 3 * PAD

        def finish_row(p, place, taps):
            valid = msk[p, 1]
            outs[p, place] = (
                taps[PAD : 2 * PAD]
                + pltpu.roll(taps[:PAD] * valid, 1, 1)
                + pltpu.roll(taps[2 * PAD :] * valid, width - 1, 1)
            )

        def predict_block(block, carry):
            start = block * RIM
            chunks = [(p, r) for r in range(0, RIM, CHUNK) for p in range(tiles)]
            products = {}

            def mix(p, r):
                value = jnp.dot(
                    wm[p], patch(p, start + r, CHUNK), preferred_element_type=jnp.float32
                )
                return value + jnp.concatenate([emb[number]] * CHUNK, axis=1)

            def hide(p, r, mixed):
                cond = mixed + feat[p, block, :, pl.ds(r * width, CHUNK * width)]
                return jnp.concatenate([silu(cond), silu(mixed)], axis=0)

            def project(p, r, both):
                z = jnp.dot(wo[p], both, preferred_element_type=jnp.float32)
                for k in range(CHUNK):
                    products[p, r + k] = z[:, k * width : (k + 1) * width]

            def part(p, a, r):
                return products[p, r][a * group : (a + 1) * group]

            def finish_rows(p, r):
                pending, above = carry[p]
                for row in range(r, r + CHUNK):
                    if row == 0:
                        taps = pending + part(p, 2, 0)
                    elif row == 1:
                        taps = above + part(p, 1, 0) + part(p, 2, 1)
                    else:
                        taps = part(p, 0, row - 2) + part(p, 1, row - 1) + part(p, 2, row)
                    finish_row(p, start + row, taps)

            mixes, hiddens = {}, {}
            for step in range(len(chunks) + 3):
                if step < len(chunks):
                    mixes[step] = mix(*chunks[step])
                if 0 <= step - 2 < len(chunks):
                    project(*chunks[step - 2], hiddens.pop(step - 2))
                if 0 <= step - 1 < len(chunks):
                    hiddens[step - 1] = hide(*chunks[step - 1], mixes.pop(step - 1))
                if 0 <= step - 3 < len(chunks):
                    finish_rows(*chunks[step - 3])
            return tuple(
                (part(p, 0, RIM - 2) + part(p, 1, RIM - 1), part(p, 0, RIM - 1))
                for p in range(tiles)
            )

        none = jnp.zeros((group, width), jnp.float32)
        carry = lax.fori_loop(0, blocks, predict_block, ((none, none),) * tiles)
        for p in range(tiles):
            finish_row(p, extent, carry[p][0])

    def start_fold(phase, buf):
        fps[buf] = jnp.zeros(fps.shape[1:], jnp.float32)

        def spread_block(block, slot, first, kind):
            halves = ([], [])
            for k in range(RIM):
                row = block * RIM + k
                first_out = outs[0, row + 1] * msk[0, kind]
                second_out = outs[1, row + 1] * msk[1, kind]
                total[buf, row] = jnp.where(lane < 3 * width // 4, first_out, 0.0) + jnp.where(
                    lane >= width // 4, second_out, 0.0
                )
                halves[0].append(second_out)
                halves[1].append(first_out)
            for group in range(2):
                part = packed(lambda k: halves[group][k], RIM * group, first)
                fps[buf, group, slot] = fps[buf, group, slot] + part

        sweep(spread_block, True)
        copies = [
            remote(total.at[buf, pl.ds(0, RIM)], fr.at[buf, 1], phase, 0, 0, -1),
            remote(total.at[buf, pl.ds(side + RIM, RIM)], fr.at[buf, 0], phase, 1, 0, 1),
        ]
        for group, dt in ((0, 1), (1, -1)):
            base = 2 + 3 * group
            mid = pl.ds(1, slots - 2)
            copies += [
                remote(fps.at[buf, group, mid], fpr.at[buf, group, mid], phase, base, dt, 0),
                remote(fps.at[buf, group, 0], fpr.at[buf, group, 0], phase, base + 1, dt, -1),
                remote(
                    fps.at[buf, group, slots - 1],
                    fpr.at[buf, group, slots - 1],
                    phase,
                    base + 2,
                    dt,
                    1,
                ),
            ]
        for copy in copies:
            copy.start()
        return copies

    def fold(buf, use):
        for group in range(2):
            fpr[buf, group, slots - 2] = fpr[buf, group, slots - 2] + fpr[buf, group, 0]
            fpr[buf, group, 1] = fpr[buf, group, 1] + fpr[buf, group, slots - 1]
        total[buf, pl.ds(RIM, RIM)] = total[buf, pl.ds(RIM, RIM)] + fr[buf, 0]
        total[buf, pl.ds(side, RIM)] = total[buf, pl.ds(side, RIM)] + fr[buf, 1]

        def fold_block(block, slot, first, _):
            kind = kind_of(block, 1, blocks - 2)
            low = fpr[buf, 0, slot]
            high = fpr[buf, 1, slot]
            scale = icov[kind]
            for k in range(RIM):
                row = block * RIM + k
                value = total[buf, row]
                value = value + jnp.where(lane < RIM, unpacked(low, 0, first + k), 0.0)
                value = value + jnp.where(
                    lane >= width - RIM, unpacked(high, RIM, first + k), 0.0
                )
                use(row, value * scale)

        sweep(fold_block, False)

    codes = [orient[my_face, my_tile * tiles + p] for p in range(tiles)]

    def per_lane(values, shape):
        return jnp.where(lax.broadcasted_iota(jnp.int32, shape, 1) < side, values[0], values[1])

    def flips_columns(code):
        return (code == 1) | (code == 2)

    picture_codes = per_lane(codes, (side, width))
    transposes = (picture_codes == 1) | (picture_codes == 3)
    source_lane = lax.broadcasted_iota(jnp.int32, (width, width), 0)
    target_lane = lax.broadcasted_iota(jnp.int32, (width, width), 1)
    tile_start = jnp.where(target_lane < side, 0, side)
    mirrored = 2 * tile_start + side - 1 - target_lane
    wanted = jnp.where(flips_columns(per_lane(codes, (width, width))), mirrored, target_lane)
    swap = jnp.where(source_lane == wanted, 1.0, 0.0).astype(jnp.bfloat16)
    swap = jnp.concatenate([swap, swap, swap], axis=0)

    def flipped(value):
        first = value.astype(jnp.bfloat16)
        rest = value - first.astype(jnp.float32)
        second = rest.astype(jnp.bfloat16)
        third = (rest - second.astype(jnp.float32)).astype(jnp.bfloat16)
        parts = jnp.concatenate([first, second, third], axis=1)
        return jnp.dot(parts, swap, preferred_element_type=jnp.float32)

    def transposed(picture):
        other = jnp.transpose(picture)
        other = jnp.concatenate([other[:side], other[side:]], axis=1)
        return jnp.where(transposes, other, picture)

    def source_row(p, row):
        return jnp.where(codes[p] >= 2, side - 1 - row, row)

    turned_rows[...] = jnp.zeros(turned_rows.shape, jnp.float32)

    def into_rows(field, ex):
        pictures = [transposed(field[channel]) for channel in range(fields)]
        pictures = flipped(jnp.concatenate(pictures, axis=0))
        for channel in range(fields):
            picture = pictures[channel * side : (channel + 1) * side]
            turned_rows[pl.ds(channel, side, stride=PAD)] = picture

        def some_rows(block, _):
            for k in range(RIM):
                row = block * RIM + k
                first = turned_rows[pl.ds(PAD * source_row(0, row), PAD)]
                second = turned_rows[pl.ds(PAD * source_row(1, row), PAD)]
                ex[row + RIM] = jnp.where(lane < side, first, second)
            return 0

        lax.fori_loop(0, side // RIM, some_rows, 0)

    fetches[0].wait()
    into_rows(given, exc)
    pl.semaphore_wait(barrier, len(around))
    cond_copies = start_exchange(exc, 0, 0)
    fetches[1].wait()
    into_rows(noisy, exs)
    state_copies = start_exchange(exs, 1, 1)
    for fetch in fetches[2:]:
        fetch.wait()
    grid_rows, grid_cols = corners.shape
    next_row = lax.rem(my_face + 1, grid_rows)
    cover_rows = []
    for p in range(tiles):
        here = my_tile * tiles + p
        beside = lax.rem(here + 1, grid_cols)
        cuts = [
            corners[my_face, here],
            corners[my_face, beside],
            corners[next_row, here],
            corners[next_row, beside],
        ]
        col = lane - (p * side - RIM)
        col = jnp.where(col < 0, col + width, jnp.where(col >= width, col - width, col))
        ones = jnp.where(col < extent, 1.0, 0.0)
        left = col < RIM
        right = (col >= side + RIM) & (col < extent)
        cut_low, cut_high = [
            jnp.where(left, cuts[k], jnp.where(right, cuts[k + 1], 0)) for k in (0, 2)
        ]
        msk[p, 0] = jnp.where(cut_low == 1, 0.0, ones)
        msk[p, 1] = ones
        msk[p, 2] = jnp.where(cut_high == 1, 0.0, ones)
        inner = lane - p * side
        left = inner < RIM
        right = inner >= side - RIM
        band = jnp.where(left | right, 1.0, 0.0)
        cut_low, cut_high = [
            jnp.where(left, cuts[k], jnp.where(right, cuts[k + 1], 1)) for k in (0, 2)
        ]
        cover_rows.append(
            (
                2.0 + band + jnp.where(cut_low == 1, 0.0, 1.0),
                1.0 + band,
                2.0 + band + jnp.where(cut_high == 1, 0.0, 1.0),
            )
        )
        tap_col = lax.broadcasted_iota(jnp.int32, (9 * PAD, 9 * fields), 0)
        tap = sum(jnp.where(tap_col >= PAD * k, 1, 0) for k in range(1, 9))
        channel = tap_col - tap * PAD
        a = jnp.where(tap >= 6, 2, jnp.where(tap >= 3, 1, 0))
        b = tap - 3 * a
        code = codes[p]
        source_a = jnp.where(
            code == 0, a, jnp.where(code == 3, b, jnp.where(code == 2, 2 - a, 2 - b))
        )
        source_b = jnp.where(
            code == 0, b, jnp.where(code == 3, 2 - a, jnp.where(code == 2, 2 - b, a))
        )
        source = (3 * source_a + source_b) * fields + channel
        place = lax.broadcasted_iota(jnp.int32, (9 * PAD, 9 * fields), 1)
        pick = jnp.where((source == place) & (channel < fields), 1.0, 0.0).astype(jnp.bfloat16)
        for weights, inner_weights in ((wm, ws_t), (wc, wc_t)):
            taps = jnp.dot(pick, inner_weights[...], preferred_element_type=jnp.float32)
            weights[p] = (0.5 * jnp.transpose(taps)).astype(jnp.bfloat16)
        taps = jnp.dot(pick, w_out[...], preferred_element_type=jnp.float32)
        wo[p] = jnp.concatenate(
            [guide_weight * taps, (1.0 - guide_weight) * taps], axis=1
        ).astype(jnp.bfloat16)
    for kind in range(3):
        cover = jnp.where(lane < side, cover_rows[0][kind], cover_rows[1][kind])
        icov[kind] = 1.0 / cover
    for number, embedding in enumerate((e1, e2)):
        spread_out = jnp.broadcast_to(0.5 * embedding[...], (width, hidden))
        emb[number] = jnp.transpose(spread_out)
    finish(cond_copies)
    windows(exc, 0, 1.0)
    features()
    finish(state_copies)
    windows(exs, 1, scale_first)
    predictions(0)
    copies = start_fold(2, 0)
    finish(copies)

    def first_use(row, slope):
        sl1[row - RIM] = slope
        exm[row] = exs[row] + step_size * slope

    fold(0, first_use)
    copies = start_exchange(exm, 3, 2)
    finish(copies)
    windows(exm, 2, scale_second)
    predictions(1)
    copies = start_fold(4, 1)
    finish(copies)

    def second_use(row, slope):
        updated[row - RIM] = exs[row] + 0.5 * step_size * (sl1[row - RIM] + slope)

    fold(1, second_use)

    def turn_block(block, _):
        rows = []
        for k in range(RIM):
            row = block * RIM + k
            first = updated[source_row(0, row)]
            second = updated[source_row(1, row)]
            rows.append(jnp.where(lane < side, first, second))
        start = pl.multiple_of(block * RIM * PAD, RIM * PAD)
        turned_rows[pl.ds(start, RIM * PAD)] = flipped(jnp.concatenate(rows, axis=0))
        return 0

    lax.fori_loop(0, side // RIM, turn_block, 0)
    for channel in range(fields):
        out[channel] = transposed(turned_rows[pl.ds(channel, side, stride=PAD)])


def local(
    noisy_state,
    conditioning,
    orient,
    corner_points,
    w_state,
    w_cond,
    w_out,
    embed_first,
    embed_second,
):
    fields, side, width = noisy_state.shape
    tiles = width // side
    extent = side + 2 * RIM
    hidden = w_state.shape[0]
    slots = (extent // RIM + 2) // 2
    f32 = jnp.float32
    vmem = pl.BlockSpec(memory_space=pltpu.VMEM)
    smem = pl.BlockSpec(memory_space=pltpu.SMEM)
    hbm = pl.BlockSpec(memory_space=pltpu.HBM)
    return pl.pallas_call(
        functools.partial(kernel, side),
        out_shape=jax.ShapeDtypeStruct((fields, side, width), f32),
        in_specs=[hbm, hbm, smem, smem, hbm, hbm, hbm, vmem, vmem],
        out_specs=vmem,
        scratch_shapes=[
            pltpu.VMEM((fields, side, width), f32),
            pltpu.VMEM((fields, side, width), f32),
            pltpu.VMEM((9 * fields, hidden), jnp.bfloat16),
            pltpu.VMEM((9 * fields, hidden), jnp.bfloat16),
            pltpu.VMEM((9 * fields, hidden), jnp.bfloat16),
            pltpu.SemaphoreType.DMA((5,)),
            pltpu.VMEM((tiles, hidden, 9 * PAD), jnp.bfloat16),
            pltpu.VMEM((tiles, hidden, 9 * PAD), jnp.bfloat16),
            pltpu.VMEM((tiles, 9 * PAD, 2 * hidden), jnp.bfloat16),
            pltpu.VMEM((2, hidden, width), f32),
            pltpu.VMEM((tiles, 3, PAD, width), f32),
            pltpu.VMEM((3, PAD, width), f32),
            pltpu.VMEM((side * PAD, width), f32),
            pltpu.VMEM((side, PAD, width), f32),
            pltpu.VMEM((extent, PAD, width), f32),
            pltpu.VMEM((extent, PAD, width), f32),
            pltpu.VMEM((extent, PAD, width), f32),
            pltpu.VMEM((tiles, 3, extent + 2, PAD, width), jnp.bfloat16),
            pltpu.VMEM((tiles, extent // RIM, hidden, RIM * width), f32),
            pltpu.VMEM((tiles, extent + 1, PAD, width), f32),
            pltpu.VMEM((2, extent, PAD, width), f32),
            pltpu.VMEM((side, PAD, width), f32),
            pltpu.VMEM((3, 2, slots, PAD, width), f32),
            pltpu.VMEM((3, 2, slots, PAD, width), f32),
            pltpu.VMEM((2, 2, RIM, PAD, width), f32),
            pltpu.VMEM((2, 2, slots, PAD, width), f32),
            pltpu.VMEM((2, 2, slots, PAD, width), f32),
            pltpu.SemaphoreType.DMA((5, 8)),
            pltpu.SemaphoreType.DMA((5, 8)),
        ],
        compiler_params=pltpu.CompilerParams(
            collective_id=0, has_side_effects=True, vmem_limit_bytes=64 * 1024 * 1024
        ),
    )(
        noisy_state,
        conditioning,
        orient,
        corner_points,
        w_state.T,
        w_cond.T,
        w_out,
        embed_first[None],
        embed_second[None],
    )


def solution(mesh):
    return jax.shard_map(
        local,
        mesh=mesh,
        in_specs=(
            P("groups", "face", "tile"),
            P("groups", "face", "tile"),
            P(),
            P(),
            P(),
            P(),
            P(),
            P(),
            P(),
        ),
        out_specs=P("groups", "face", "tile"),
        check_vma=False,
    )
```

```python
import functools
import math

import jax
import jax.numpy as jnp
from jax import lax
from jax.experimental import pallas as pl
from jax.experimental.pallas import tpu as pltpu
from jax.sharding import PartitionSpec as P

RIM = 8
PAD = 16
CHUNK = 4
MESH = pl.DeviceIdType.MESH

guide_weight = 2.0
sigma_first = 1.0
sigma_second = 0.6
step_size = sigma_second - sigma_first
scale_first = 1.0 / math.sqrt(1.0 + sigma_first**2)
scale_second = 1.0 / math.sqrt(1.0 + sigma_second**2)


def silu(value):
    return (value + value * jnp.tanh(value)).astype(jnp.bfloat16)


def kernel(
    side,
    noisy_in, given_in, orient, corners, ws_in, wc_in, w_out_in, e1, e2,
    out,
    noisy, given, ws_t, wc_t, w_out, fetched,
    wm, wc, wo, emb, msk, icov, turned_rows, updated,
    exs, exc, exm, win, feat, outs, total, sl1,
    ps, pr, fr, fps, fpr,
    send, recv,
):
    fetches = [
        pltpu.make_async_copy(source, target, fetched.at[number])
        for number, (source, target) in enumerate(
            (
                (given_in, given),
                (noisy_in, noisy),
                (ws_in, ws_t),
                (wc_in, wc_t),
                (w_out_in, w_out),
            )
        )
    ]
    for fetch in fetches:
        fetch.start()
    fields, _, width = noisy.shape
    hidden = w_out.shape[1]
    extent = side + 2 * RIM
    blocks = extent // RIM
    tiles = width // side
    n_tile = lax.axis_size("tile")
    n_face = lax.axis_size("face")
    my_tile = lax.axis_index("tile")
    my_face = lax.axis_index("face")

    def device(d_tile, d_face):
        return {
            "tile": lax.rem(my_tile + d_tile + n_tile, n_tile),
            "face": lax.rem(my_face + d_face + n_face, n_face),
        }

    around = [(dt, df) for dt in (-1, 0, 1) for df in (-1, 0, 1) if (dt, df) != (0, 0)]
    barrier = pltpu.get_barrier_semaphore()
    for dt, df in around:
        pl.semaphore_signal(barrier, inc=1, device_id=device(dt, df), device_id_type=MESH)
    lane = lax.broadcasted_iota(jnp.int32, (PAD, width), 1)
    slots = (blocks + 2) // 2

    def remote(src, dst, phase, number, dt, df):
        return pltpu.make_async_remote_copy(
            src_ref=src,
            dst_ref=dst,
            send_sem=send.at[phase, number],
            recv_sem=recv.at[phase, number],
            device_id=device(dt, df),
            device_id_type=MESH,
        )

    def packed(load, shift, first):
        value = jnp.zeros((PAD, width), jnp.float32)
        for k in range(RIM):
            place = k + first
            moved = pltpu.roll(load(k), (shift + RIM * place) % width, 1)
            inside = (lane >= RIM * place) & (lane < RIM * (place + 1))
            value = jnp.where(inside, moved, value)
        return value

    def unpacked(slot, shift, place):
        return pltpu.roll(slot, (-shift - RIM * place) % width, 1)

    def kind_of(block, low, high):
        return jnp.where(block == low, 0, jnp.where(block == high, 2, 1))

    def sweep(visit, ends):
        if ends:
            visit(0, 0, RIM, 0)

        def pair(slot, _):
            visit(2 * slot - 1, slot, 0, 1)
            visit(2 * slot, slot, RIM, 1)
            return 0

        lax.fori_loop(1, slots - 1, pair, 0)
        if ends:
            visit(blocks - 1, slots - 1, 0, 2)

    def start_exchange(ex, phase, buf):
        def pack_block(block, slot, first, _):
            for group in range(2):
                part = packed(lambda k: ex[block * RIM + k], RIM * group, first)
                ps[buf, group, slot] = ps[buf, group, slot] + part

        ps[buf] = jnp.zeros(ps.shape[1:], jnp.float32)
        sweep(pack_block, False)
        copies = [
            remote(ex.at[pl.ds(RIM, RIM)], ex.at[pl.ds(side + RIM, RIM)], phase, 0, 0, -1),
            remote(ex.at[pl.ds(side, RIM)], ex.at[pl.ds(0, RIM)], phase, 1, 0, 1),
        ]
        for group, dt in ((0, -1), (1, 1)):
            base = 2 + 3 * group
            mid = pl.ds(1, slots - 2)
            copies += [
                remote(ps.at[buf, group, mid], pr.at[buf, group, mid], phase, base, dt, 0),
                remote(
                    ps.at[buf, group, 1], pr.at[buf, group, slots - 1], phase, base + 1, dt, -1
                ),
                remote(
                    ps.at[buf, group, slots - 2], pr.at[buf, group, 0], phase, base + 2, dt, 1
                ),
            ]
        for copy in copies:
            copy.start()
        return copies

    def finish(copies):
        for copy in copies:
            copy.wait()

    def windows(ex, buf, scale):
        for p in range(tiles):
            for b in range(3):
                win[p, b, 0] = jnp.zeros((PAD, width), jnp.bfloat16)
                win[p, b, extent + 1] = jnp.zeros((PAD, width), jnp.bfloat16)

        def window_block(block, slot, first, kind):
            after = pr[buf, 0, slot]
            before = pr[buf, 1, slot]
            for k in range(RIM):
                row = block * RIM + k
                body = ex[row]
                left = jnp.where(lane >= width - RIM, unpacked(before, RIM, first + k), body)
                right = jnp.where(lane < RIM, unpacked(after, 0, first + k), body)
                for p, picture in ((0, left), (1, right)):
                    value = jnp.where(msk[p, kind] > 0, scale * picture, 0.0)
                    win[p, 0, row + 1] = pltpu.roll(value, 1, 1).astype(jnp.bfloat16)
                    win[p, 1, row + 1] = value.astype(jnp.bfloat16)
                    win[p, 2, row + 1] = pltpu.roll(value, width - 1, 1).astype(jnp.bfloat16)

        sweep(window_block, True)

    def patch(p, first_row, count):
        taps = []
        for a in range(3):
            for b in range(3):
                rows = win[p, b, pl.ds(first_row + a, count)]
                taps.append(jnp.concatenate([rows[r] for r in range(count)], axis=1))
        return jnp.concatenate(taps, axis=0)

    def features():
        def feature_block(block, _):
            for p in range(tiles):
                feat[p, block] = jnp.dot(
                    wc[p], patch(p, block * RIM, RIM), preferred_element_type=jnp.float32
                )
            return 0

        lax.fori_loop(0, blocks, feature_block, 0)

    def predictions(number):
        group = 3 * PAD

        def finish_row(p, place, taps):
            valid = msk[p, 1]
            outs[p, place] = (
                taps[PAD : 2 * PAD]
                + pltpu.roll(taps[:PAD] * valid, 1, 1)
                + pltpu.roll(taps[2 * PAD :] * valid, width - 1, 1)
            )

        def predict_block(block, carry):
            start = block * RIM
            chunks = [(p, r) for r in range(0, RIM, CHUNK) for p in range(tiles)]
            products = {}

            def mix(p, r):
                value = jnp.dot(
                    wm[p], patch(p, start + r, CHUNK), preferred_element_type=jnp.float32
                )
                return value + jnp.concatenate([emb[number]] * CHUNK, axis=1)

            def hide(p, r, mixed):
                cond = mixed + feat[p, block, :, pl.ds(r * width, CHUNK * width)]
                return jnp.concatenate([silu(cond), silu(mixed)], axis=0)

            def project(p, r, both):
                z = jnp.dot(wo[p], both, preferred_element_type=jnp.float32)
                for k in range(CHUNK):
                    products[p, r + k] = z[:, k * width : (k + 1) * width]

            def part(p, a, r):
                return products[p, r][a * group : (a + 1) * group]

            def finish_rows(p, r):
                pending, above = carry[p]
                for row in range(r, r + CHUNK):
                    if row == 0:
                        taps = pending + part(p, 2, 0)
                    elif row == 1:
                        taps = above + part(p, 1, 0) + part(p, 2, 1)
                    else:
                        taps = part(p, 0, row - 2) + part(p, 1, row - 1) + part(p, 2, row)
                    finish_row(p, start + row, taps)

            mixes, hiddens = {}, {}
            for step in range(len(chunks) + 3):
                if step < len(chunks):
                    mixes[step] = mix(*chunks[step])
                if 0 <= step - 2 < len(chunks):
                    project(*chunks[step - 2], hiddens.pop(step - 2))
                if 0 <= step - 1 < len(chunks):
                    hiddens[step - 1] = hide(*chunks[step - 1], mixes.pop(step - 1))
                if 0 <= step - 3 < len(chunks):
                    finish_rows(*chunks[step - 3])
            return tuple(
                (part(p, 0, RIM - 2) + part(p, 1, RIM - 1), part(p, 0, RIM - 1))
                for p in range(tiles)
            )

        none = jnp.zeros((group, width), jnp.float32)
        carry = lax.fori_loop(0, blocks, predict_block, ((none, none),) * tiles)
        for p in range(tiles):
            finish_row(p, extent, carry[p][0])

    def start_fold(phase, buf):
        fps[buf] = jnp.zeros(fps.shape[1:], jnp.float32)

        def spread_block(block, slot, first, kind):
            halves = ([], [])
            for k in range(RIM):
                row = block * RIM + k
                first_out = outs[0, row + 1] * msk[0, kind]
                second_out = outs[1, row + 1] * msk[1, kind]
                total[buf, row] = jnp.where(lane < 3 * width // 4, first_out, 0.0) + jnp.where(
                    lane >= width // 4, second_out, 0.0
                )
                halves[0].append(second_out)
                halves[1].append(first_out)
            for group in range(2):
                part = packed(lambda k: halves[group][k], RIM * group, first)
                fps[buf, group, slot] = fps[buf, group, slot] + part

        sweep(spread_block, True)
        copies = [
            remote(total.at[buf, pl.ds(0, RIM)], fr.at[buf, 1], phase, 0, 0, -1),
            remote(total.at[buf, pl.ds(side + RIM, RIM)], fr.at[buf, 0], phase, 1, 0, 1),
        ]
        for group, dt in ((0, 1), (1, -1)):
            base = 2 + 3 * group
            mid = pl.ds(1, slots - 2)
            copies += [
                remote(fps.at[buf, group, mid], fpr.at[buf, group, mid], phase, base, dt, 0),
                remote(fps.at[buf, group, 0], fpr.at[buf, group, 0], phase, base + 1, dt, -1),
                remote(
                    fps.at[buf, group, slots - 1],
                    fpr.at[buf, group, slots - 1],
                    phase,
                    base + 2,
                    dt,
                    1,
                ),
            ]
        for copy in copies:
            copy.start()
        return copies

    def fold(buf, use):
        for group in range(2):
            fpr[buf, group, slots - 2] = fpr[buf, group, slots - 2] + fpr[buf, group, 0]
            fpr[buf, group, 1] = fpr[buf, group, 1] + fpr[buf, group, slots - 1]
        total[buf, pl.ds(RIM, RIM)] = total[buf, pl.ds(RIM, RIM)] + fr[buf, 0]
        total[buf, pl.ds(side, RIM)] = total[buf, pl.ds(side, RIM)] + fr[buf, 1]

        def fold_block(block, slot, first, _):
            kind = kind_of(block, 1, blocks - 2)
            low = fpr[buf, 0, slot]
            high = fpr[buf, 1, slot]
            scale = icov[kind]
            for k in range(RIM):
                row = block * RIM + k
                value = total[buf, row]
                value = value + jnp.where(lane < RIM, unpacked(low, 0, first + k), 0.0)
                value = value + jnp.where(
                    lane >= width - RIM, unpacked(high, RIM, first + k), 0.0
                )
                use(row, value * scale)

        sweep(fold_block, False)

    codes = [orient[my_face, my_tile * tiles + p] for p in range(tiles)]

    def per_lane(values, shape):
        return jnp.where(lax.broadcasted_iota(jnp.int32, shape, 1) < side, values[0], values[1])

    def flips_columns(code):
        return (code == 1) | (code == 2)

    picture_codes = per_lane(codes, (side, width))
    transposes = (picture_codes == 1) | (picture_codes == 3)
    source_lane = lax.broadcasted_iota(jnp.int32, (width, width), 0)
    target_lane = lax.broadcasted_iota(jnp.int32, (width, width), 1)
    tile_start = jnp.where(target_lane < side, 0, side)
    mirrored = 2 * tile_start + side - 1 - target_lane
    wanted = jnp.where(flips_columns(per_lane(codes, (width, width))), mirrored, target_lane)
    swap = jnp.where(source_lane == wanted, 1.0, 0.0).astype(jnp.bfloat16)
    swap = jnp.concatenate([swap, swap, swap], axis=0)

    def flipped(value):
        first = value.astype(jnp.bfloat16)
        rest = value - first.astype(jnp.float32)
        second = rest.astype(jnp.bfloat16)
        third = (rest - second.astype(jnp.float32)).astype(jnp.bfloat16)
        parts = jnp.concatenate([first, second, third], axis=1)
        return jnp.dot(parts, swap, preferred_element_type=jnp.float32)

    def transposed(picture):
        other = jnp.transpose(picture)
        other = jnp.concatenate([other[:side], other[side:]], axis=1)
        return jnp.where(transposes, other, picture)

    def source_row(p, row):
        return jnp.where(codes[p] >= 2, side - 1 - row, row)

    turned_rows[...] = jnp.zeros(turned_rows.shape, jnp.float32)

    def into_rows(field, ex):
        pictures = [transposed(field[channel]) for channel in range(fields)]
        pictures = flipped(jnp.concatenate(pictures, axis=0))
        for channel in range(fields):
            picture = pictures[channel * side : (channel + 1) * side]
            turned_rows[pl.ds(channel, side, stride=PAD)] = picture

        def some_rows(block, _):
            for k in range(RIM):
                row = block * RIM + k
                first = turned_rows[pl.ds(PAD * source_row(0, row), PAD)]
                second = turned_rows[pl.ds(PAD * source_row(1, row), PAD)]
                ex[row + RIM] = jnp.where(lane < side, first, second)
            return 0

        lax.fori_loop(0, side // RIM, some_rows, 0)

    fetches[0].wait()
    into_rows(given, exc)
    pl.semaphore_wait(barrier, len(around))
    cond_copies = start_exchange(exc, 0, 0)
    fetches[1].wait()
    into_rows(noisy, exs)
    state_copies = start_exchange(exs, 1, 1)
    for fetch in fetches[2:]:
        fetch.wait()
    grid_rows, grid_cols = corners.shape
    next_row = lax.rem(my_face + 1, grid_rows)
    cover_rows = []
    for p in range(tiles):
        here = my_tile * tiles + p
        beside = lax.rem(here + 1, grid_cols)
        cuts = [
            corners[my_face, here],
            corners[my_face, beside],
            corners[next_row, here],
            corners[next_row, beside],
        ]
        col = lane - (p * side - RIM)
        col = jnp.where(col < 0, col + width, jnp.where(col >= width, col - width, col))
        ones = jnp.where(col < extent, 1.0, 0.0)
        left = col < RIM
        right = (col >= side + RIM) & (col < extent)
        cut_low, cut_high = [
            jnp.where(left, cuts[k], jnp.where(right, cuts[k + 1], 0)) for k in (0, 2)
        ]
        msk[p, 0] = jnp.where(cut_low == 1, 0.0, ones)
        msk[p, 1] = ones
        msk[p, 2] = jnp.where(cut_high == 1, 0.0, ones)
        inner = lane - p * side
        left = inner < RIM
        right = inner >= side - RIM
        band = jnp.where(left | right, 1.0, 0.0)
        cut_low, cut_high = [
            jnp.where(left, cuts[k], jnp.where(right, cuts[k + 1], 1)) for k in (0, 2)
        ]
        cover_rows.append(
            (
                2.0 + band + jnp.where(cut_low == 1, 0.0, 1.0),
                1.0 + band,
                2.0 + band + jnp.where(cut_high == 1, 0.0, 1.0),
            )
        )
        tap_col = lax.broadcasted_iota(jnp.int32, (9 * PAD, 9 * fields), 0)
        tap = sum(jnp.where(tap_col >= PAD * k, 1, 0) for k in range(1, 9))
        channel = tap_col - tap * PAD
        a = jnp.where(tap >= 6, 2, jnp.where(tap >= 3, 1, 0))
        b = tap - 3 * a
        code = codes[p]
        source_a = jnp.where(
            code == 0, a, jnp.where(code == 3, b, jnp.where(code == 2, 2 - a, 2 - b))
        )
        source_b = jnp.where(
            code == 0, b, jnp.where(code == 3, 2 - a, jnp.where(code == 2, 2 - b, a))
        )
        source = (3 * source_a + source_b) * fields + channel
        place = lax.broadcasted_iota(jnp.int32, (9 * PAD, 9 * fields), 1)
        pick = jnp.where((source == place) & (channel < fields), 1.0, 0.0).astype(jnp.bfloat16)
        for weights, inner_weights in ((wm, ws_t), (wc, wc_t)):
            taps = jnp.dot(pick, inner_weights[...], preferred_element_type=jnp.float32)
            weights[p] = (0.5 * jnp.transpose(taps)).astype(jnp.bfloat16)
        taps = jnp.dot(pick, w_out[...], preferred_element_type=jnp.float32)
        wo[p] = jnp.concatenate(
            [guide_weight * taps, (1.0 - guide_weight) * taps], axis=1
        ).astype(jnp.bfloat16)
    for kind in range(3):
        cover = jnp.where(lane < side, cover_rows[0][kind], cover_rows[1][kind])
        icov[kind] = 1.0 / cover
    for number, embedding in enumerate((e1, e2)):
        spread_out = jnp.broadcast_to(0.5 * embedding[...], (width, hidden))
        emb[number] = jnp.transpose(spread_out)
    finish(cond_copies)
    windows(exc, 0, 1.0)
    features()
    finish(state_copies)
    windows(exs, 1, scale_first)
    predictions(0)
    copies = start_fold(2, 0)
    finish(copies)

    def first_use(row, slope):
        sl1[row - RIM] = slope
        exm[row] = exs[row] + step_size * slope

    fold(0, first_use)
    copies = start_exchange(exm, 3, 2)
    finish(copies)
    windows(exm, 2, scale_second)
    predictions(1)
    copies = start_fold(4, 1)
    finish(copies)

    def second_use(row, slope):
        updated[row - RIM] = exs[row] + 0.5 * step_size * (sl1[row - RIM] + slope)

    fold(1, second_use)

    def turn_block(block, _):
        rows = []
        for k in range(RIM):
            row = block * RIM + k
            first = updated[source_row(0, row)]
            second = updated[source_row(1, row)]
            rows.append(jnp.where(lane < side, first, second))
        start = pl.multiple_of(block * RIM * PAD, RIM * PAD)
        turned_rows[pl.ds(start, RIM * PAD)] = flipped(jnp.concatenate(rows, axis=0))
        return 0

    lax.fori_loop(0, side // RIM, turn_block, 0)
    for channel in range(fields):
        out[channel] = transposed(turned_rows[pl.ds(channel, side, stride=PAD)])


def local(
    noisy_state,
    conditioning,
    orient,
    corner_points,
    w_state,
    w_cond,
    w_out,
    embed_first,
    embed_second,
):
    fields, side, width = noisy_state.shape
    tiles = width // side
    extent = side + 2 * RIM
    hidden = w_state.shape[0]
    slots = (extent // RIM + 2) // 2
    f32 = jnp.float32
    vmem = pl.BlockSpec(memory_space=pltpu.VMEM)
    smem = pl.BlockSpec(memory_space=pltpu.SMEM)
    hbm = pl.BlockSpec(memory_space=pltpu.HBM)
    return pl.pallas_call(
        functools.partial(kernel, side),
        out_shape=jax.ShapeDtypeStruct((fields, side, width), f32),
        in_specs=[hbm, hbm, smem, smem, hbm, hbm, hbm, vmem, vmem],
        out_specs=vmem,
        scratch_shapes=[
            pltpu.VMEM((fields, side, width), f32),
            pltpu.VMEM((fields, side, width), f32),
            pltpu.VMEM((9 * fields, hidden), jnp.bfloat16),
            pltpu.VMEM((9 * fields, hidden), jnp.bfloat16),
            pltpu.VMEM((9 * fields, hidden), jnp.bfloat16),
            pltpu.SemaphoreType.DMA((5,)),
            pltpu.VMEM((tiles, hidden, 9 * PAD), jnp.bfloat16),
            pltpu.VMEM((tiles, hidden, 9 * PAD), jnp.bfloat16),
            pltpu.VMEM((tiles, 9 * PAD, 2 * hidden), jnp.bfloat16),
            pltpu.VMEM((2, hidden, width), f32),
            pltpu.VMEM((tiles, 3, PAD, width), f32),
            pltpu.VMEM((3, PAD, width), f32),
            pltpu.VMEM((side * PAD, width), f32),
            pltpu.VMEM((side, PAD, width), f32),
            pltpu.VMEM((extent, PAD, width), f32),
            pltpu.VMEM((extent, PAD, width), f32),
            pltpu.VMEM((extent, PAD, width), f32),
            pltpu.VMEM((tiles, 3, extent + 2, PAD, width), jnp.bfloat16),
            pltpu.VMEM((tiles, extent // RIM, hidden, RIM * width), f32),
            pltpu.VMEM((tiles, extent + 1, PAD, width), f32),
            pltpu.VMEM((2, extent, PAD, width), f32),
            pltpu.VMEM((side, PAD, width), f32),
            pltpu.VMEM((3, 2, slots, PAD, width), f32),
            pltpu.VMEM((3, 2, slots, PAD, width), f32),
            pltpu.VMEM((2, 2, RIM, PAD, width), f32),
            pltpu.VMEM((2, 2, slots, PAD, width), f32),
            pltpu.VMEM((2, 2, slots, PAD, width), f32),
            pltpu.SemaphoreType.DMA((5, 8)),
            pltpu.SemaphoreType.DMA((5, 8)),
        ],
        compiler_params=pltpu.CompilerParams(
            collective_id=0, has_side_effects=True, vmem_limit_bytes=64 * 1024 * 1024
        ),
    )(
        noisy_state,
        conditioning,
        orient,
        corner_points,
        w_state.T,
        w_cond.T,
        w_out,
        embed_first[None],
        embed_second[None],
    )


def solution(mesh):
    return jax.shard_map(
        local,
        mesh=mesh,
        in_specs=(
            P("groups", "face", "tile"),
            P("groups", "face", "tile"),
            P(),
            P(),
            P(),
            P(),
            P(),
            P(),
            P(),
        ),
        out_specs=P("groups", "face", "tile"),
        check_vma=False,
    )
```
